128 devices in a mesh: dp: 4 (over y), ctx: 32 (over z, x, core).
Axes of the slice: x: 4, y: 4, z: 4, core: 2. Of those that a mesh axis runs over, the one named last changes fastest.
Arguments:
- tokens: bfloat16 [4, 4096, 2048], P('dp', 'ctx'), may hold values from -6 to 6
- queries: bfloat16 [4, 4096, 2048], P('dp', 'ctx'), may hold values from -6 to 6
- values: bfloat16 [4, 4096, 2048], P('dp', 'ctx'), may hold values from -6 to 6
- key_weight: bfloat16 [2048, 2048], replicated, may hold values from -0.125 to 0.125
- grad_out: bfloat16 [4, 4096, 2048], P('dp', 'ctx'), may hold values from -6 to 6
Outputs:
- attended: bfloat16 [4, 4096, 2048], P('dp', 'ctx')
- grad_tokens: bfloat16 [4, 4096, 2048], P('dp', 'ctx')
- grad_queries: bfloat16 [4, 4096, 2048], P('dp', 'ctx')
- grad_values: bfloat16 [4, 4096, 2048], P('dp', 'ctx')
- grad_key_weight: float32 [2048, 2048], P('ctx')
The draws below stay inside these ranges and needn't reach their ends.
All inputs are finite; a program needn't handle non-finite values.
Results may differ from the reference program's by a relative error of at most 0.024.
Values may be sent and summed in bfloat16 or wider, within the bound.
A program may use at most 128 MiB of HBM per device.

```python
import jax
import jax.numpy as jnp
from jax import lax

H = 16
DH = 128
D = 2048
TOK_DEV = 128
COARSE = 64
LEVELS = 5
SEQ = 4096
DOCS = 4
N_CTX = 32


def steps_of(rng, extent, shards, smallest, top_value):
    loudness = 1.0
    for axis_at, parts in shards:
        draws = jax.random.uniform(jax.random.fold_in(jax.random.fold_in(rng, 6), axis_at), (parts,), jnp.float32, smallest / len(shards), top_value / len(shards))
        loudness = loudness * jnp.repeat(jnp.exp(draws), extent[axis_at] // parts).reshape((-1,) + (1,) * (len(extent) - 1 - axis_at))
    return loudness


def bell_draw(rng, shape, deviation, limit, pieces=(), held_as=jnp.bfloat16):
    gain = steps_of(rng, shape, pieces, -0.22, 0.18) if pieces else 1.0
    result = jax.random.normal(rng, shape, jnp.float32) * deviation * gain
    return jnp.minimum(jnp.maximum(result, -limit), limit).astype(held_as)


def setup_inputs(seed: int = 0) -> dict:
    splits = jax.random.split(jax.random.key(seed), 6)
    return {
        "tokens": bell_draw(splits[0], (DOCS, SEQ, D), 1.0, 6.0, ((0, 4), (1, 32))),
        "queries": bell_draw(splits[1], (DOCS, SEQ, D), 1.0, 6.0, ((0, 4), (1, 32))),
        "values": bell_draw(splits[2], (DOCS, SEQ, D), 1.0, 6.0, ((0, 4), (1, 32))),
        "key_weight": bell_draw(splits[3], (D, D), D ** -0.5, 0.125),
        "grad_out": bell_draw(splits[4], (DOCS, SEQ, D), 1.0, 6.0, ((0, 4), (1, 32))),
    }


def reference(tokens, queries, values, key_weight, grad_out):
    blocks = N_CTX
    span0 = TOK_DEV // COARSE
    scale = DH ** -0.5
    high = lax.Precision.HIGHEST
    coarse_rows = LEVELS * COARSE

    def one_block(item):
        query_b, key_b, value_b, grad_b, coarse_kb, coarse_vb = item
        query_f = query_b.astype(jnp.float32).reshape(TOK_DEV, H, DH)
        key_h = key_b.astype(jnp.float32).reshape(TOK_DEV, H, DH)
        value_h = value_b.astype(jnp.float32).reshape(TOK_DEV, H, DH)
        grad_f = grad_b.astype(jnp.float32).reshape(TOK_DEV, H, DH)
        coarse_k = coarse_kb.reshape(coarse_rows, H, DH)
        coarse_v = coarse_vb.reshape(coarse_rows, H, DH)
        local_s = jnp.einsum('qhd,khd->hqk', query_f, key_h, precision=high) * scale
        coarse_s = jnp.einsum('qhd,khd->hqk', query_f, coarse_k, precision=high) * scale
        local_e = jnp.exp(local_s)
        coarse_e = jnp.exp(coarse_s)
        denom = local_e.sum(-1, keepdims=True) + coarse_e.sum(-1, keepdims=True)
        local_p = local_e / denom
        coarse_p = coarse_e / denom
        local_pb = local_p.astype(jnp.bfloat16).astype(jnp.float32)
        out_f = (jnp.einsum('hqk,khd->qhd', local_pb, value_h, precision=high)
                 + jnp.einsum('hqk,khd->qhd', coarse_p, coarse_v, precision=high))
        local_dp = jnp.einsum('qhd,khd->hqk', grad_f, value_h, precision=high)
        coarse_dp = jnp.einsum('qhd,khd->hqk', grad_f, coarse_v, precision=high)
        delta = jnp.einsum('qhd,qhd->hq', grad_f, out_f, precision=high)[..., None]
        local_ds = local_p * (local_dp - delta) * scale
        coarse_ds = coarse_p * (coarse_dp - delta) * scale
        local_dsb = local_ds.astype(jnp.bfloat16).astype(jnp.float32)
        grad_q = (jnp.einsum('hqk,khd->qhd', local_dsb, key_h, precision=high)
                  + jnp.einsum('hqk,khd->qhd', coarse_ds, coarse_k, precision=high))
        local_dk = jnp.einsum('hqk,qhd->khd', local_dsb, query_f, precision=high)
        local_dv = jnp.einsum('hqk,qhd->khd', local_pb, grad_f, precision=high)
        coarse_dk = jnp.einsum('hqk,qhd->khd', coarse_ds, query_f, precision=high)
        coarse_dv = jnp.einsum('hqk,qhd->khd', coarse_p, grad_f, precision=high)
        return (out_f.astype(jnp.bfloat16).reshape(TOK_DEV, D),
                grad_q.astype(jnp.bfloat16).reshape(TOK_DEV, D),
                local_dk.reshape(TOK_DEV, D), local_dv.reshape(TOK_DEV, D),
                coarse_dk.reshape(coarse_rows, D), coarse_dv.reshape(coarse_rows, D))

    def per_doc(item):
        x_doc, q_doc, v_doc, g_doc = item
        keys = jnp.dot(x_doc, key_weight, preferred_element_type=jnp.float32).astype(jnp.bfloat16)
        key_f = keys.reshape(blocks, TOK_DEV, D).astype(jnp.float32)
        value_f = v_doc.reshape(blocks, TOK_DEV, D).astype(jnp.float32)
        part_k = []
        part_v = []
        for level in range(LEVELS):
            span = (2 ** level) * span0
            groups = blocks >> level
            sum_k = key_f.reshape(groups, COARSE, span, D).mean(2)
            sum_v = value_f.reshape(groups, COARSE, span, D).mean(2)
            partner = (jnp.arange(blocks, dtype=jnp.int32) >> level) ^ 1
            part_k.append(sum_k[partner])
            part_v.append(sum_v[partner])
        coarse_k = jnp.concatenate(part_k, 1)
        coarse_v = jnp.concatenate(part_v, 1)
        attended, grad_q, local_dk, local_dv, coarse_dk, coarse_dv = lax.map(
            one_block,
            (q_doc.reshape(blocks, TOK_DEV, D), keys.reshape(blocks, TOK_DEV, D),
             v_doc.reshape(blocks, TOK_DEV, D), g_doc.reshape(blocks, TOK_DEV, D),
             coarse_k, coarse_v))
        for level in range(LEVELS):
            span = (2 ** level) * span0
            groups = blocks >> level
            owner = jnp.arange(groups, dtype=jnp.int32) ^ 1
            piece_k = coarse_dk[:, level * COARSE:(level + 1) * COARSE].reshape(groups, 2 ** level, COARSE, D).sum(1)[owner]
            piece_v = coarse_dv[:, level * COARSE:(level + 1) * COARSE].reshape(groups, 2 ** level, COARSE, D).sum(1)[owner]
            local_dk = local_dk + jnp.broadcast_to(piece_k[:, :, None, :] / span, (groups, COARSE, span, D)).reshape(blocks, TOK_DEV, D)
            local_dv = local_dv + jnp.broadcast_to(piece_v[:, :, None, :] / span, (groups, COARSE, span, D)).reshape(blocks, TOK_DEV, D)
        grad_k = local_dk.astype(jnp.bfloat16)
        grad_v = local_dv.astype(jnp.bfloat16)
        grad_x = jnp.dot(grad_k.reshape(SEQ, D), key_weight.T, preferred_element_type=jnp.float32).astype(jnp.bfloat16)

        def add_block(total, item_block):
            x_block, k_block = item_block
            partial_sum = jnp.dot(x_block.T, k_block, preferred_element_type=jnp.float32).astype(jnp.bfloat16)
            partial_sum = lax.optimization_barrier(partial_sum)
            return total + partial_sum.astype(jnp.float32), None

        weight_sum, _ = lax.scan(add_block, jnp.zeros((D, D), jnp.float32),
                                 (x_doc.reshape(blocks, TOK_DEV, D), grad_k))
        return (attended.reshape(SEQ, D), grad_x, grad_q.reshape(SEQ, D), grad_v.reshape(SEQ, D), weight_sum)

    attended, grad_x, grad_q, grad_v, weight_sums = lax.map(per_doc, (tokens, queries, values, grad_out))
    return attended, grad_x, grad_q, grad_v, weight_sums.sum(0)
```

```python
import math

import jax
import jax.numpy as jnp
import numpy as np
from jax import lax
from jax.experimental import pallas as pl
from jax.experimental.pallas import tpu as pltpu
from jax.sharding import PartitionSpec as P

DH = 128
TOK = 128
D = 2048
HALF = D // 2
GROUPS = 4
GC = HALF // GROUPS
SCALE = DH ** (-0.5)
BF = jnp.bfloat16
F32 = jnp.float32
MESH = pl.DeviceIdType.MESH
N_SEM = 160


def matrices():
    pool = np.zeros((224, 384), np.float32)
    for tok in range(256):
        pool[tok // 2, tok] = 0.5
        pool[128 + tok // 4, tok] = 0.25
        pool[192 + tok // 8, tok] = 0.125
    rise = np.zeros((96, 384), np.float32)
    for row in range(64):
        rise[row // 4, row] = 0.25
        rise[64 + row // 8, row] = 0.125
        rise[16 + row // 4, 128 + row] = 0.25
        rise[72 + row // 8, 128 + row] = 0.125
        rise[32 + row // 2, 192 + row] = 0.5
        rise[80 + row // 4, 192 + row] = 0.25
    third = np.zeros((64, 128), np.float32)
    for row in range(64):
        third[row, row] = 1.0
        third[row, 64 + row // 2] = 0.5
        third[row, 96 + row // 2] = 0.5
    back = np.zeros((128, 384), np.float32)
    for row in range(64):
        back[row, :128] = third[16 + row // 4] * 0.25
        back[64 + row, :128] = third[32 + row // 2] * 0.5
    spread = np.zeros((256, 384), np.float32)
    for tok in range(256):
        spread[tok, tok // 2] = 0.5
        spread[tok, 128 + tok // 4] = 0.25
        spread[tok, 192 + tok // 8] = 0.125
        spread[tok, 224 + tok // 8] = 0.125
        spread[tok, 256:384] = third[tok // 16] / 16
    return np.concatenate([pool, rise, back, spread], 0)


def flipped(place, k):
    if k == 0:
        return place
    if k == 1:
        return place + 1 - 2 * (place % 2)
    if k == 2:
        return place + 2 - 4 * (place // 2)
    return 3 - place


def nn(a, b):
    return lax.dot_general(a, b, (((1,), (0,)), ((), ())), preferred_element_type=F32)


def nt(a, b):
    return lax.dot_general(a, b, (((1,), (1,)), ((), ())), preferred_element_type=F32)


def tn(a, b):
    return lax.dot_general(a, b, (((0,), (0,)), ((), ())), preferred_element_type=F32)


SCRATCH = dict(
    xa=((4 * 256, D), BF),
    wv=((GROUPS, D, GC), BF),
    qv=((256, HALF), BF),
    gv=((256, HALF), BF),
    kl=((2, 192, HALF), BF),
    vl=((2, 192, HALF), BF),
    cc=((2, 256, HALF), BF),
    sp=((2, 96, HALF), BF),
    sz=((2, 96, HALF), BF),
    dcb=((2, 256, HALF), BF),
    dcf=((2, 128, HALF), F32),
    rb=((2, 384, HALF), BF),
    sx=((2, 128, HALF), BF),
    ld=((2, 256, HALF), F32),
    gkv=((2, 256, HALF), BF),
    ao=((256, HALF), BF),
    qo=((256, HALF), BF),
    gy=((2, 4, 256, 128), BF),
    gt=((128, 1024), BF),
    rs=((2, 4, 4, 128, 128), BF),
    ra=((2, 3, 4, 128, 128), BF),
    tf=((2, 4, 128, 128), F32),
    tb=((2, 4, 128, 128), BF),
    rz=((2, 3, 128, 128), BF),
    fo=((2, 128, 128), BF),
    ow=((64, D), BF),
    gxf=((128, D), F32),
    gxs=((128, D), BF),
    gxr=((128, D), BF),
    gxo=((128, D), BF),
    pp=((704, 384), BF),
)


def kernel(x_h, q_h, v_h, w_h, g_h, p_h, att_h, gx_h, gq_h, gvo_h, gw_h, *rest):
    s = dict(zip(SCRATCH, rest[: len(SCRATCH)]))
    ssem, rsem = rest[len(SCRATCH) :]
    xa, wv, qv, gv, kl, vl, cc = (s[n] for n in ("xa", "wv", "qv", "gv", "kl", "vl", "cc"))
    sp, sz, dcb, dcf, rb, sx, ld = (s[n] for n in ("sp", "sz", "dcb", "dcf", "rb", "sx", "ld"))
    gkv, ao, qo, gy, gt = (s[n] for n in ("gkv", "ao", "qo", "gy", "gt"))
    rs, ra, tf, tb, rz, fo, ow = (s[n] for n in ("rs", "ra", "tf", "tb", "rz", "fo", "ow"))
    gxf, gxs, gxr, gxo, pp = (s[n] for n in ("gxf", "gxs", "gxr", "gxo", "pp"))

    y = lax.axis_index("dp")
    ctx = lax.axis_index("ctx")
    core = ctx % 2
    xx = (ctx // 2) % 4
    zz = ctx // 8
    mate = (y, ctx + 1 - 2 * core)
    along_x = [(y, zz * 8 + flipped(xx, k) * 2 + core) for k in range(4)]
    along_z = [(y, flipped(zz, k) * 8 + xx * 2 + core) for k in range(4)]
    along_y = [(flipped(y, k), ctx) for k in range(4)]
    cross_y = [(flipped(y, k), mate[1]) for k in range(4)]
    mine = pl.multiple_of(core * HALF, HALF)
    theirs = pl.multiple_of((1 - core) * HALF, HALF)

    count = [0]
    sent = []
    stored = []

    def remote(src, dst, device):
        at = count[0]
        count[0] += 1
        copy = pltpu.make_async_remote_copy(
            src_ref=src, dst_ref=dst, send_sem=ssem.at[at], recv_sem=rsem.at[at], device_id=device, device_id_type=MESH
        )
        copy.start()
        sent.append(copy)
        return copy

    def local(src, dst):
        at = count[0]
        count[0] += 1
        copy = pltpu.make_async_copy(src, dst, ssem.at[at])
        copy.start()
        return copy

    def arrive(copies):
        for copy in copies:
            copy.wait_recv()

    def cols(j):
        return pl.ds(j * GC, GC)

    in_x = local(x_h, xa.at[0:128])
    in_v = local(v_h.at[:, pl.ds(mine, HALF)], vl.at[0, 0:128])
    in_p = local(p_h, pp)
    in_w = [local(w_h.at[:, pl.ds(pl.multiple_of(mine + j * GC, GC), GC)], wv.at[j]) for j in range(GROUPS)]
    in_q = local(q_h.at[:, pl.ds(mine, HALF)], qv.at[0:128])
    in_g = local(g_h.at[:, pl.ds(mine, HALF)], gv.at[0:128])

    peers = [mate] + along_x[1:] + along_z[1:] + along_y[1:] + cross_y[1:]
    barrier = pltpu.get_barrier_semaphore()
    for peer in peers:
        pl.semaphore_signal(barrier, inc=1, device_id=peer, device_id_type=MESH)
    pl.semaphore_wait(barrier, len(peers))

    m_v = remote(v_h.at[:, pl.ds(theirs, HALF)], vl.at[1, 0:128], mate)
    m_x = remote(x_h, xa.at[128:256], mate)
    m_q = remote(q_h.at[:, pl.ds(theirs, HALF)], qv.at[128:256], mate)
    m_g = remote(g_h.at[:, pl.ds(theirs, HALF)], gv.at[128:256], mate)
    y_x = [None] + [remote(x_h, xa.at[k * 256 : k * 256 + 128], along_y[k]) for k in (1, 2, 3)]

    def pooled(kv, ref, j, both):
        rows = nn(pp[0:224, 0:256], both).astype(BF)
        ref[1, 128:192, cols(j)] = rows[0:64]
        ref[0, 128:192, cols(j)] = rows[64:128]
        sp[kv, :, cols(j)] = rows[128:224]

    def send_x(kv, at):
        return [
            remote(sp.at[kv, 0:64, at], cc.at[kv, 0:64, at], along_x[1]),
            remote(sp.at[kv, 64:96, at], cc.at[kv, 64:96, at], along_x[2]),
            remote(sp.at[kv, 64:96, at], cc.at[kv, 96:128, at], along_x[3]),
        ]

    def rise(kv, j):
        rows = nn(pp[224:320, 0:64], sp[kv, 0:64, cols(j)]) + nn(pp[224:320, 128:256], cc[kv, 0:128, cols(j)])
        sz[kv, :, cols(j)] = rows.astype(BF)

    def send_z(kv, at):
        return [
            remote(sz.at[kv, 0:64, at], cc.at[kv, 128:192, at], along_z[1]),
            remote(sz.at[kv, 64:96, at], cc.at[kv, 192:224, at], along_z[2]),
            remote(sz.at[kv, 64:96, at], cc.at[kv, 224:256, at], along_z[3]),
        ]

    everything = pl.ds(0, HALF)

    in_p.wait()
    in_v.wait()
    m_v.wait_recv()
    for j in range(GROUPS):
        pooled(1, vl, j, jnp.concatenate([vl[0, 0:128, cols(j)], vl[1, 0:128, cols(j)]], 0))
    vx = send_x(1, everything)

    in_x.wait()
    m_x.wait_recv()
    kx = []
    for j in range(GROUPS):
        in_w[j].wait()
        keys = nn(xa[0:256, :], wv[j]).astype(BF)
        kl[0, 0:128, cols(j)] = keys[0:128]
        kl[1, 0:128, cols(j)] = keys[128:256]
        pooled(0, kl, j, keys)
        kx.append(send_x(0, cols(j)))

    arrive(vx)
    for j in range(GROUPS):
        rise(1, j)
    vz = send_z(1, everything)
    kz = []
    for j in range(GROUPS):
        arrive(kx[j])
        rise(0, j)
        kz.append(send_z(0, cols(j)))

    in_q.wait()
    in_g.wait()
    m_q.wait_recv()
    m_g.wait_recv()

    def head(at):
        c = pl.ds(at, DH)
        q = qv[:, c]
        g = gv[:, c]
        ck = cc[0, :, c]
        cv = cc[1, :, c]
        rate = SCALE * math.log2(math.e)
        e1 = jnp.exp2(nt(q, ck) * rate)
        total = jnp.sum(e1, -1, keepdims=True)
        pair = [slice(0, 128), slice(128, 256)]
        e0 = [jnp.exp2(nt(q[pair[b]], kl[b, :, c]) * rate) for b in (0, 1)]
        total = total + jnp.concatenate([jnp.sum(e, -1, keepdims=True) for e in e0], 0)
        inverse = 1.0 / (total * 0.25)
        p1 = e1 * inverse
        p0 = [e0[b] * inverse[pair[b]] for b in (0, 1)]
        p1b = p1.astype(BF)
        p0b = [p.astype(BF) for p in p0]
        out = (nn(p1b, cv) + jnp.concatenate([nn(p0b[b], vl[b, :, c]) for b in (0, 1)], 0)) * 0.25
        ao[:, c] = out.astype(BF)
        delta = jnp.sum(g.astype(F32) * out, -1, keepdims=True)
        d1 = (p1 * (nt(g, cv) - delta)).astype(BF)
        d0 = [(p0[b] * (nt(g[pair[b]], vl[b, :, c]) - delta[pair[b]])).astype(BF) for b in (0, 1)]
        fold = SCALE * 0.25
        dq = (nn(d1, ck) + jnp.concatenate([nn(d0[b], kl[b, :, c]) for b in (0, 1)], 0)) * fold
        qo[:, c] = dq.astype(BF)
        dck = tn(d1, q) * fold
        dcv = tn(p1b, g) * 0.25
        dcf[0, :, c] = dck[0:128]
        dcf[1, :, c] = dcv[0:128]
        dcb[0, 128:256, c] = dck[128:256].astype(BF)
        dcb[1, 128:256, c] = dcv[128:256].astype(BF)
        for b in (0, 1):
            dk = tn(d0[b], q[pair[b]]) * fold
            dv = tn(p0b[b], g[pair[b]]) * 0.25
            ld[0, pair[b], c] = dk[0:128]
            ld[1, pair[b], c] = dv[0:128]
            other = slice(64 - 64 * b, 128 - 64 * b)
            rb[0, other, c] = dk[128:192].astype(BF)
            rb[1, other, c] = dv[128:192].astype(BF)

    def attend(j):
        arrive(kz[j])

        def step(i, carry):
            head(pl.multiple_of(j * GC + i * DH, DH))
            return carry

        lax.fori_loop(0, GC // DH, step, 0)
        at = cols(j)
        return [
            remote(dcb.at[:, 128:192, at], rb.at[:, 256:320, at], along_z[1]),
            remote(dcb.at[:, 192:224, at], rb.at[:, 320:352, at], along_z[2]),
            remote(dcb.at[:, 224:256, at], rb.at[:, 352:384, at], along_z[3]),
        ]

    def return_x(j, copies):
        arrive(copies)
        at = cols(j)
        for kv in (0, 1):
            sx[kv, :, at] = (dcf[kv, :, at] + nn(pp[320:448, 0:128], rb[kv, 256:384, at])).astype(BF)
        return [
            remote(sx.at[:, 0:64, at], rb.at[:, 128:192, at], along_x[1]),
            remote(sx.at[:, 64:96, at], rb.at[:, 192:224, at], along_x[2]),
            remote(sx.at[:, 96:128, at], rb.at[:, 224:256, at], along_x[3]),
        ]

    def finish(j, copies):
        arrive(copies)
        at = cols(j)
        for kv in (0, 1):
            gkv[kv, :, at] = (ld[kv, :, at] + nn(pp[448:704, :], rb[kv, :, at])).astype(BF)

    def send_y(half):
        copies = []
        for k in (1, 2, 3):
            at = pl.ds(pl.multiple_of((half * 4 + flipped(y, k)) * DH, DH), DH)
            copies.append(remote(gkv.at[0, :, at], gy.at[half, k], along_y[k]))
        return copies

    def forward(k):
        y_x[k].wait_recv()
        return remote(xa.at[k * 256 : k * 256 + 128], xa.at[k * 256 + 128 : k * 256 + 256], mate)

    def weights(half, copies):
        own = pl.ds(pl.multiple_of((half * 4 + y) * DH, DH), DH)
        gt[:, 0:256] = gkv[0, :, own].T
        arrive(copies)
        for k in (1, 2, 3):
            gt[:, k * 256 : (k + 1) * 256] = gy[half, k].T

        def step(i, carry):
            part = nn(gt[...], xa[:, pl.ds(pl.multiple_of(i * 256, 256), 256)]).astype(BF)
            z_at = i // 2
            x_at = 2 * (i % 2)
            if half == 0:
                rs[0, x_at, z_at] = part[:, 0:128]
                rs[0, x_at + 1, z_at] = part[:, 128:256]
            else:
                rs[1, z_at, x_at] = part[:, 0:128]
                rs[1, z_at, x_at + 1] = part[:, 128:256]
            return carry

        lax.fori_loop(0, 8, step, 0)
        place, line = (xx, along_x) if half == 0 else (zz, along_z)
        return [remote(rs.at[half, flipped(place, k)], ra.at[half, k - 1], line[k]) for k in (1, 2, 3)]

    def second(half, copies):
        place = xx if half == 0 else zz
        arrive(copies)
        total = rs[half, place].astype(F32)
        for k in range(3):
            total = total + ra[half, k].astype(F32)
        tf[half] = total
        tb[half] = total.astype(BF)
        place, line = (zz, along_z) if half == 0 else (xx, along_x)
        return [remote(tb.at[half, flipped(place, k)], rz.at[half, k - 1], line[k]) for k in (1, 2, 3)]

    def third(half, copies):
        place = zz if half == 0 else xx
        arrive(copies)
        total = tf[half, place]
        for k in range(3):
            total = total + rz[half, k].astype(F32)
        fo[half] = total.T.astype(BF)
        at = pl.ds(pl.multiple_of((core * 8 + half * 4 + y) * DH, DH), DH)
        same = pl.ds(pl.multiple_of(core * 64, 64), 64)
        cross = pl.ds(pl.multiple_of(64 - core * 64, 64), 64)
        ow[:, at] = fo[half, same, :]
        return [remote(fo.at[half, same], ow.at[:, at], along_y[k]) for k in (1, 2, 3)] + [
            remote(fo.at[half, cross], ow.at[:, at], cross_y[k]) for k in range(4)
        ]

    def give(staged, out):
        stored.append(local(staged.at[0:128], out.at[:, pl.ds(mine, HALF)]))
        return remote(staged.at[128:256], out.at[:, pl.ds(mine, HALF)], mate)

    arrive(vz)
    bz0 = attend(0)
    bz1 = attend(1)
    bx0 = return_x(0, bz0)
    f1 = forward(1)
    bz2 = attend(2)
    bx1 = return_x(1, bz1)
    f3 = forward(3)
    finish(0, bx0)
    bz3 = attend(3)
    given = [give(ao, att_h), give(qo, gq_h)]
    bx2 = return_x(2, bz2)
    finish(1, bx1)
    gy0 = send_y(0)
    f2 = forward(2)
    bx3 = return_x(3, bz3)
    finish(2, bx2)
    arrive([f1, f2, f3])
    ax0 = weights(0, gy0)
    finish(3, bx3)
    gy1 = send_y(1)
    given.append(give(gkv.at[1], gvo_h))
    bx0 = second(0, ax0)
    ax1 = weights(1, gy1)

    def partial(i, carry):
        at = pl.ds(pl.multiple_of(i * 256, 256), 256)
        total = nt(gkv[0, :, cols(0)], wv[0, at, :])
        for j in range(1, GROUPS):
            total = total + nt(gkv[0, :, cols(j)], wv[j, at, :])
        gxf[:, at] = total[0:128]
        gxs[:, at] = total[128:256].astype(BF)
        return carry

    lax.fori_loop(0, 8, partial, 0)
    gxc = remote(gxs, gxr, mate)
    last0 = third(0, bx0)
    bx1 = second(1, ax1)
    gxc.wait_recv()
    gxo[...] = (gxf[...] + gxr[...].astype(F32)).astype(BF)
    stored.append(local(gxo, gx_h))
    last1 = third(1, bx1)
    arrive(last0)
    arrive(last1)
    stored.append(local(ow, gw_h))
    arrive(given)
    for copy in stored:
        copy.wait()
    for copy in sent:
        copy.wait_send()


def body(tokens, queries, values, key_weight, grad_out):
    anywhere = pl.BlockSpec(memory_space=pl.ANY)
    block = jax.ShapeDtypeStruct((TOK, D), BF)
    att, gx, gq, gv, gw = pl.pallas_call(
        kernel,
        out_shape=[block] * 4 + [jax.ShapeDtypeStruct((64, D), BF)],
        in_specs=[anywhere] * 6,
        out_specs=[anywhere] * 5,
        scratch_shapes=[pltpu.VMEM(shape, dtype) for shape, dtype in SCRATCH.values()]
        + [pltpu.SemaphoreType.DMA((N_SEM,)), pltpu.SemaphoreType.DMA((N_SEM,))],
        compiler_params=pltpu.CompilerParams(
            collective_id=0, has_side_effects=True, vmem_limit_bytes=56 * 1024 * 1024
        ),
        name="hierarchical_attention",
    )(tokens[0], queries[0], values[0], key_weight, grad_out[0], jnp.asarray(matrices(), BF))
    return att[None], gx[None], gq[None], gv[None], gw.astype(F32)


def solution(mesh):
    split = P("dp", "ctx", None)
    return jax.shard_map(
        body,
        mesh=mesh,
        in_specs=(split, split, split, P(), split),
        out_specs=(split, split, split, split, P("ctx", None)),
        check_vma=False,
    )
```

```python
import math

import jax
import jax.numpy as jnp
import numpy as np
from jax import lax
from jax.experimental import pallas as pl
from jax.experimental.pallas import tpu as pltpu
from jax.sharding import PartitionSpec as P

DH = 128
TOK = 128
D = 2048
HALF = D // 2
GROUPS = 4
GC = HALF // GROUPS
SCALE = DH ** (-0.5)
BF = jnp.bfloat16
F32 = jnp.float32
MESH = pl.DeviceIdType.MESH
N_SEM = 208


def matrices():
    pool = np.zeros((112, 384), np.float32)
    for tok in range(128):
        pool[tok // 2, tok] = 0.5
        pool[64 + tok // 4, tok] = 0.25
        pool[96 + tok // 8, tok] = 0.125
    rise = np.zeros((96, 384), np.float32)
    for row in range(64):
        rise[row // 4, row] = 0.25
        rise[64 + row // 8, row] = 0.125
        rise[16 + row // 4, 128 + row] = 0.25
        rise[72 + row // 8, 128 + row] = 0.125
        rise[32 + row // 2, 192 + row] = 0.5
        rise[80 + row // 4, 192 + row] = 0.25
    third = np.zeros((64, 128), np.float32)
    for row in range(64):
        third[row, row] = 1.0
        third[row, 64 + row // 2] = 0.5
        third[row, 96 + row // 2] = 0.5
    back = np.zeros((128, 384), np.float32)
    for row in range(64):
        back[row, :128] = third[16 + row // 4] * 0.25
        back[64 + row, :128] = third[32 + row // 2] * 0.5
    spread = np.zeros((256, 384), np.float32)
    for tok in range(256):
        spread[tok, tok // 2] = 0.5
        spread[tok, 128 + tok // 4] = 0.25
        spread[tok, 192 + tok // 8] = 0.125
        spread[tok, 224 + tok // 8] = 0.125
        spread[tok, 256:384] = third[tok // 16] / 16
    return np.concatenate([pool, rise, back, spread], 0)


def flipped(place, k):
    if k == 0:
        return place
    if k == 1:
        return place + 1 - 2 * (place % 2)
    if k == 2:
        return place + 2 - 4 * (place // 2)
    return 3 - place


def nn(a, b):
    return lax.dot_general(a, b, (((1,), (0,)), ((), ())), preferred_element_type=F32)


def nt(a, b):
    return lax.dot_general(a, b, (((1,), (1,)), ((), ())), preferred_element_type=F32)


def tn(a, b):
    return lax.dot_general(a, b, (((0,), (0,)), ((), ())), preferred_element_type=F32)


SCRATCH = dict(
    xa=((4 * 256, D), BF),
    wv=((2, GROUPS, D, GC), BF),
    qv=((256, HALF), BF),
    gv=((256, HALF), BF),
    kl=((2, 192, HALF), BF),
    vl=((2, 192, HALF), BF),
    kt=((128, HALF), BF),
    vt=((128, HALF), BF),
    lo=((2, 64, HALF), BF),
    cc=((2, 256, HALF), BF),
    sp=((2, 2, 48, HALF), BF),
    sz=((2, 96, HALF), BF),
    dcb=((2, 256, HALF), BF),
    dcf=((2, 128, HALF), F32),
    rb=((2, 384, HALF), BF),
    sx=((2, 128, HALF), BF),
    ld=((2, 256, HALF), F32),
    gkv=((2, 256, HALF), BF),
    ao=((256, HALF), BF),
    qo=((256, HALF), BF),
    gs=((GROUPS, 256, 256), BF),
    gt=((GROUPS, 64, 1024), BF),
    rs=((GROUPS, 2, 4, 4, 32, 128), BF),
    ra=((GROUPS, 2, 3, 4, 32, 128), BF),
    tf=((GROUPS, 2, 4, 32, 128), F32),
    tb=((GROUPS, 2, 4, 32, 128), BF),
    rz=((GROUPS, 2, 3, 32, 128), BF),
    fo=((GROUPS, 64, 128), BF),
    ow=((D, 128), BF),
    gxf=((128, D), F32),
    gxs=((128, D), BF),
    gxr=((128, D), BF),
    pp=((592, 384), BF),
)


def kernel(x_h, q_h, v_h, w_h, g_h, p_h, att_o, gx_o, gq_o, gv_o, gw_o, *rest):
    s = dict(zip(SCRATCH, rest[: len(SCRATCH)]))
    ssem, rsem = rest[len(SCRATCH) :]
    xa, wv, qv, gv, kl, vl, kt, vt, lo = (s[n] for n in ("xa", "wv", "qv", "gv", "kl", "vl", "kt", "vt", "lo"))
    cc, sp, sz, dcb, dcf, rb, sx, ld = (s[n] for n in ("cc", "sp", "sz", "dcb", "dcf", "rb", "sx", "ld"))
    gkv, ao, qo, gs, gt = (s[n] for n in ("gkv", "ao", "qo", "gs", "gt"))
    rs, ra, tf, tb, rz, fo, ow = (s[n] for n in ("rs", "ra", "tf", "tb", "rz", "fo", "ow"))
    gxf, gxs, gxr, pp = (s[n] for n in ("gxf", "gxs", "gxr", "pp"))

    y = lax.axis_index("dp")
    ctx = lax.axis_index("ctx")
    core = ctx % 2
    xx = (ctx // 2) % 4
    zz = ctx // 8
    mate = (y, ctx + 1 - 2 * core)
    along_x = [(y, zz * 8 + flipped(xx, k) * 2 + core) for k in range(4)]
    cross_x = [(y, zz * 8 + flipped(xx, k) * 2 + 1 - core) for k in range(4)]
    along_z = [(y, flipped(zz, k) * 8 + xx * 2 + core) for k in range(4)]
    along_y = [(flipped(y, k), ctx) for k in range(4)]
    cross_y = [(flipped(y, k), mate[1]) for k in range(4)]
    mine = pl.multiple_of(core * HALF, HALF)
    theirs = pl.multiple_of((1 - core) * HALF, HALF)

    peers = [mate] + along_x[1:] + cross_x[1:] + along_z[1:] + along_y[1:] + cross_y[1:]
    barrier = pltpu.get_barrier_semaphore()
    for peer in peers:
        pl.semaphore_signal(barrier, inc=1, device_id=peer, device_id_type=MESH)

    count = [0]
    sent = []
    stored = []

    def remote(src, dst, device):
        at = count[0]
        count[0] += 1
        copy = pltpu.make_async_remote_copy(
            src_ref=src, dst_ref=dst, send_sem=ssem.at[at], recv_sem=rsem.at[at], device_id=device, device_id_type=MESH
        )
        copy.start()
        sent.append(copy)
        return copy

    def local(src, dst):
        at = count[0]
        count[0] += 1
        copy = pltpu.make_async_copy(src, dst, ssem.at[at])
        copy.start()
        return copy

    def arrive(copies):
        for copy in copies:
            copy.wait_recv()

    def cols(j):
        return pl.ds(j * GC, GC)

    in_x = local(x_h, xa.at[0:128])
    in_p = local(p_h, pp)
    in_v = [local(v_h.at[:, pl.ds(mine, HALF)], vl.at[0, 0:128]), local(v_h.at[:, pl.ds(theirs, HALF)], vt)]
    in_w = [
        [local(w_h.at[:, pl.ds(pl.multiple_of(side + j * GC, GC), GC)], wv.at[h, j]) for h, side in enumerate((mine, theirs))]
        for j in range(GROUPS)
    ]
    in_q = local(q_h.at[:, pl.ds(mine, HALF)], qv.at[0:128])
    in_g = local(g_h.at[:, pl.ds(mine, HALF)], gv.at[0:128])

    def pooled(kv, ref, h, j, rows_in):
        rows = nn(pp[0:112, 0:128], rows_in).astype(BF)
        sp[h, kv, :, cols(j)] = rows[64:112]
        if h == 0:
            ref[1, 128:192, cols(j)] = rows[0:64]
            lo[kv, 0:32, cols(j)] = rows[64:96]

    in_p.wait()
    for copy in in_v:
        copy.wait()
    for j in range(GROUPS):
        pooled(1, vl, 0, j, vl[0, 0:128, cols(j)])
        pooled(1, vl, 1, j, vt[:, cols(j)])
    in_x.wait()
    for j in range(GROUPS):
        for h in (0, 1):
            in_w[j][h].wait()
            keys = nn(xa[0:128, :], wv[h, j]).astype(BF)
            if h == 0:
                kl[0, 0:128, cols(j)] = keys
            else:
                kt[:, cols(j)] = keys
            pooled(0, kl, h, j, keys)

    pl.semaphore_wait(barrier, len(peers))

    def send_x(j):
        at = cols(j)
        copies = []
        for h, line in ((0, along_x), (1, cross_x)):
            first = sp.at[h, :, 0:32, at]
            second = sp.at[h, :, 32:48, at]
            copies.append(remote(first, cc.at[:, 32 * h : 32 * h + 32, at], line[1]))
            copies.append(remote(second, cc.at[:, 64 + 16 * h : 80 + 16 * h, at], line[2]))
            copies.append(remote(second, cc.at[:, 96 + 16 * h : 112 + 16 * h, at], line[3]))
        return copies

    fx = [send_x(0)]
    m_k = remote(kt, kl.at[1, 0:128], mate)
    m_v = remote(vt, vl.at[1, 0:128], mate)
    for j in range(1, GROUPS):
        fx.append(send_x(j))
    m_q = remote(q_h.at[:, pl.ds(theirs, HALF)], qv.at[128:256], mate)
    m_g = remote(g_h.at[:, pl.ds(theirs, HALF)], gv.at[128:256], mate)
    y_x = [None] + [remote(x_h, xa.at[k * 256 : k * 256 + 128], along_y[k]) for k in (1, 2, 3)]
    m_x = remote(x_h, xa.at[128:256], mate)

    arrive([m_k, m_v])
    for kv, ref in ((0, kl), (1, vl)):
        for j in range(GROUPS):
            rows = nn(pp[0:96, 0:128], ref[1, 0:128, cols(j)]).astype(BF)
            ref[0, 128:192, cols(j)] = rows[0:64]
            lo[kv, 32:64, cols(j)] = rows[64:96]

    def rise(j):
        arrive(fx[j])
        at = cols(j)
        for kv in (0, 1):
            rows = nn(pp[112:208, 0:64], lo[kv, :, at]) + nn(pp[112:208, 128:256], cc[kv, 0:128, at])
            sz[kv, :, at] = rows.astype(BF)
        return [
            remote(sz.at[:, 0:64, at], cc.at[:, 128:192, at], along_z[1]),
            remote(sz.at[:, 64:96, at], cc.at[:, 192:224, at], along_z[2]),
            remote(sz.at[:, 64:96, at], cc.at[:, 224:256, at], along_z[3]),
        ]

    def head(at):
        c = pl.ds(at, DH)
        q = qv[:, c]
        g = gv[:, c]
        ck = cc[0, :, c]
        cv = cc[1, :, c]
        rate = SCALE * math.log2(math.e)
        e1 = jnp.exp2(nt(q, ck) * rate)
        total = jnp.sum(e1, -1, keepdims=True)
        pair = [slice(0, 128), slice(128, 256)]
        e0 = [jnp.exp2(nt(q[pair[b]], kl[b, :, c]) * rate) for b in (0, 1)]
        total = total + jnp.concatenate([jnp.sum(e, -1, keepdims=True) for e in e0], 0)
        inverse = 1.0 / (total * 0.25)
        p1 = e1 * inverse
        p0 = [e0[b] * inverse[pair[b]] for b in (0, 1)]
        p1b = p1.astype(BF)
        p0b = [p.astype(BF) for p in p0]
        out = (nn(p1b, cv) + jnp.concatenate([nn(p0b[b], vl[b, :, c]) for b in (0, 1)], 0)) * 0.25
        ao[:, c] = out.astype(BF)
        delta = jnp.sum(g.astype(F32) * out, -1, keepdims=True)
        d1 = (p1 * (nt(g, cv) - delta)).astype(BF)
        d0 = [(p0[b] * (nt(g[pair[b]], vl[b, :, c]) - delta[pair[b]])).astype(BF) for b in (0, 1)]
        fold = SCALE * 0.25
        dq = (nn(d1, ck) + jnp.concatenate([nn(d0[b], kl[b, :, c]) for b in (0, 1)], 0)) * fold
        qo[:, c] = dq.astype(BF)
        dck = tn(d1, q) * fold
        dcv = tn(p1b, g) * 0.25
        dcf[0, :, c] = dck[0:128]
        dcf[1, :, c] = dcv[0:128]
        dcb[0, 128:256, c] = dck[128:256].astype(BF)
        dcb[1, 128:256, c] = dcv[128:256].astype(BF)
        for b in (0, 1):
            dk = tn(d0[b], q[pair[b]]) * fold
            dv = tn(p0b[b], g[pair[b]]) * 0.25
            ld[0, pair[b], c] = dk[0:128]
            ld[1, pair[b], c] = dv[0:128]
            other = slice(64 - 64 * b, 128 - 64 * b)
            rb[0, other, c] = dk[128:192].astype(BF)
            rb[1, other, c] = dv[128:192].astype(BF)

    def attend(j, copies):
        arrive(copies)

        def step(i, carry):
            head(pl.multiple_of(j * GC + i * DH, DH))
            return carry

        lax.fori_loop(0, GC // DH, step, 0)
        at = cols(j)
        return [
            remote(dcb.at[:, 128:192, at], rb.at[:, 256:320, at], along_z[1]),
            remote(dcb.at[:, 192:224, at], rb.at[:, 320:352, at], along_z[2]),
            remote(dcb.at[:, 224:256, at], rb.at[:, 352:384, at], along_z[3]),
        ]

    def return_x(j, copies):
        arrive(copies)
        at = cols(j)
        for kv in (0, 1):
            sx[kv, :, at] = (dcf[kv, :, at] + nn(pp[208:336, 0:128], rb[kv, 256:384, at])).astype(BF)
        return [
            remote(sx.at[:, 0:64, at], rb.at[:, 128:192, at], along_x[1]),
            remote(sx.at[:, 64:96, at], rb.at[:, 192:224, at], along_x[2]),
            remote(sx.at[:, 96:128, at], rb.at[:, 224:256, at], along_x[3]),
        ]

    def finish(j, copies):
        arrive(copies)
        at = cols(j)
        for kv in (0, 1):
            total = ld[kv, :, at] + nn(pp[336:592, :], rb[kv, :, at])
            gkv[kv, :, at] = total.astype(BF)
            if kv == 0:
                gs[j] = total.T.astype(BF)
        quarter = [pl.ds(pl.multiple_of(flipped(y, k) * 64, 64), 64) for k in range(4)]
        copies = [remote(gs.at[j, quarter[k]], gt.at[j, :, k * 256 : (k + 1) * 256], along_y[k]) for k in (1, 2, 3)]
        gt[j, :, 0:256] = gs[j, quarter[0], :]
        return copies

    def forward(k):
        arrive([y_x[k]])
        return remote(xa.at[k * 256 : k * 256 + 128], xa.at[k * 256 + 128 : k * 256 + 256], mate)

    lines = ((xx, along_x), (zz, along_z))

    def weights(j, copies):
        arrive(copies)

        def step(i, carry):
            part = nn(gt[j], xa[:, pl.ds(pl.multiple_of(i * 256, 256), 256)]).astype(BF)
            z_at = i // 2
            x_at = 2 * (i % 2)
            for n in (0, 1):
                rs[j, 0, x_at + n, z_at] = part[0:32, n * 128 : n * 128 + 128]
                rs[j, 1, z_at, x_at + n] = part[32:64, n * 128 : n * 128 + 128]
            return carry

        lax.fori_loop(0, 8, step, 0)
        return [
            remote(rs.at[j, d, flipped(lines[d][0], k)], ra.at[j, d, k - 1], lines[d][1][k]) for k in (1, 2, 3) for d in (0, 1)
        ]

    def second(j, copies):
        arrive(copies)
        copies = []
        for d in (0, 1):
            total = rs[j, d, lines[d][0]].astype(F32)
            for k in range(3):
                total = total + ra[j, d, k].astype(F32)
            tf[j, d] = total
            tb[j, d] = total.astype(BF)
            place, line = lines[1 - d]
            copies += [remote(tb.at[j, d, flipped(place, k)], rz.at[j, d, k - 1], line[k]) for k in (1, 2, 3)]
        return copies

    def third(j, copies):
        arrive(copies)
        for d in (0, 1):
            total = tf[j, d, lines[1 - d][0]]
            for k in range(3):
                total = total + rz[j, d, k].astype(F32)
            fo[j, d * 32 : d * 32 + 32] = total.astype(BF)
        at = pl.ds(pl.multiple_of(core * HALF + j * GC + y * 64, 64), 64)
        copies = [remote(fo.at[j], ow.at[at], along_y[k]) for k in (1, 2, 3)]
        copies += [remote(fo.at[j], ow.at[at], cross_y[k]) for k in range(4)]
        ow[at, :] = fo[j]
        return copies

    def assemble(j, copies):
        arrive(copies)
        for side in (0, 1):
            at = pl.ds(side * HALF + j * GC, GC)
            turned = ow[at, :].astype(F32).T
            gw_o[:, at] = jnp.where(core == 0, turned[0:64], turned[64:128])

    def give(staged, out):
        stored.append(local(staged.at[0:128], out.at[:, pl.ds(mine, HALF)]))
        return remote(staged.at[128:256], out.at[:, pl.ds(mine, HALF)], mate)

    def partial(i, carry):
        at = pl.ds(pl.multiple_of(i * 256, 256), 256)
        total = nt(gkv[0, :, cols(0)], wv[0, 0, at, :])
        for j in range(1, GROUPS):
            total = total + nt(gkv[0, :, cols(j)], wv[0, j, at, :])
        gxf[:, at] = total[0:128]
        gxs[:, at] = total[128:256].astype(BF)
        return carry

    fz = [rise(0), rise(1)]
    in_q.wait()
    in_g.wait()
    arrive([m_q, m_g])
    bz0 = attend(0, fz[0])
    fz.append(rise(2))
    bz1 = attend(1, fz[1])
    fz.append(rise(3))
    bx0 = return_x(0, bz0)
    bz2 = attend(2, fz[2])
    bx1 = return_x(1, bz1)
    gy0 = finish(0, bx0)
    bz3 = attend(3, fz[3])
    given = [give(ao, att_o), give(qo, gq_o)]
    bx2 = return_x(2, bz2)
    gy1 = finish(1, bx1)
    fw = [forward(1), forward(3)]
    bx3 = return_x(3, bz3)
    gy2 = finish(2, bx2)
    fw.append(forward(2))
    gy3 = finish(3, bx3)
    given.append(give(gkv.at[1], gv_o))
    arrive([m_x])
    arrive(fw)
    wa0 = weights(0, gy0)
    wa1 = weights(1, gy1)
    wa2 = weights(2, gy2)
    wa3 = weights(3, gy3)
    lax.fori_loop(0, 4, partial, 0)
    wb0 = second(0, wa0)
    wb1 = second(1, wa1)
    lax.fori_loop(4, 8, partial, 0)
    gxc = remote(gxs, gxr, mate)
    wb2 = second(2, wa2)
    wb3 = second(3, wa3)
    wc0 = third(0, wb0)
    wc1 = third(1, wb1)
    wc2 = third(2, wb2)
    wc3 = third(3, wb3)
    arrive([gxc])
    gx_o[...] = (gxf[...] + gxr[...].astype(F32)).astype(BF)
    assemble(0, wc0)
    assemble(1, wc1)
    assemble(2, wc2)
    assemble(3, wc3)
    arrive(given)
    for copy in stored:
        copy.wait()
    for copy in sent:
        copy.wait_send()


def hand_over(*refs):
    sources, outs, sem = refs[:5], refs[5:10], refs[10]
    copies = [pltpu.make_async_copy(src, out, sem.at[i]) for i, (src, out) in enumerate(zip(sources, outs))]
    for copy in copies:
        copy.start()
    for copy in copies:
        copy.wait()


def body(tokens, queries, values, key_weight, grad_out):
    anywhere = pl.BlockSpec(memory_space=pl.ANY)
    block = jax.ShapeDtypeStruct((TOK, D), BF)
    shapes = [block] * 4 + [jax.ShapeDtypeStruct((64, D), F32)]
    held = [pltpu.VMEM(shape.shape, shape.dtype) for shape in shapes]
    results = pl.pallas_call(
        kernel,
        out_shape=held,
        in_specs=[anywhere] * 6,
        out_specs=[pl.BlockSpec(memory_space=pltpu.VMEM)] * 5,
        scratch_shapes=[pltpu.VMEM(shape, dtype) for shape, dtype in SCRATCH.values()]
        + [pltpu.SemaphoreType.DMA((N_SEM,)), pltpu.SemaphoreType.DMA((N_SEM,))],
        compiler_params=pltpu.CompilerParams(
            collective_id=0, has_side_effects=True, vmem_limit_bytes=56 * 1024 * 1024
        ),
        name="hierarchical_attention",
    )(tokens[0], queries[0], values[0], key_weight, grad_out[0], jnp.asarray(matrices(), BF))
    att, gx, gq, gv, gw = pl.pallas_call(
        hand_over,
        out_shape=shapes,
        in_specs=[pl.BlockSpec(memory_space=pltpu.VMEM)] * 5,
        out_specs=[anywhere] * 5,
        scratch_shapes=[pltpu.SemaphoreType.DMA((5,))],
        name="hand_over",
    )(*[pltpu.with_memory_space_constraint(r, pltpu.VMEM) for r in results])
    return att[None], gx[None], gq[None], gv[None], gw


def solution(mesh):
    split = P("dp", "ctx", None)
    return jax.shard_map(
        body,
        mesh=mesh,
        in_specs=(split, split, split, P(), split),
        out_specs=(split, split, split, split, P("ctx", None)),
        check_vma=False,
    )
```

```python
import math

import jax
import jax.numpy as jnp
import numpy as np
from jax import lax
from jax.experimental import pallas as pl
from jax.experimental.pallas import tpu as pltpu
from jax.sharding import PartitionSpec as P

DH = 128
TOK = 128
D = 2048
HALF = D // 2
GROUPS = 4
GC = HALF // GROUPS
HEADS = 8
PARTS = ((0, 6), (6, 8))
SCALE = DH ** (-0.5)
BF = jnp.bfloat16
F32 = jnp.float32
MESH = pl.DeviceIdType.MESH
SENDS = 48
LANDINGS = 60


def matrices():
    pool = np.zeros((112, 384), np.float32)
    for tok in range(128):
        pool[tok // 2, tok] = 0.5
        pool[64 + tok // 4, tok] = 0.25
        pool[96 + tok // 8, tok] = 0.125
    rise = np.zeros((96, 384), np.float32)
    for row in range(64):
        rise[row // 4, row] = 0.25
        rise[64 + row // 8, row] = 0.125
        rise[16 + row // 4, 128 + row] = 0.25
        rise[72 + row // 8, 128 + row] = 0.125
        rise[32 + row // 2, 192 + row] = 0.5
        rise[80 + row // 4, 192 + row] = 0.25
    third = np.zeros((64, 128), np.float32)
    for row in range(64):
        third[row, row] = 1.0
        third[row, 64 + row // 2] = 0.5
        third[row, 96 + row // 2] = 0.5
    back = np.zeros((128, 384), np.float32)
    for row in range(64):
        back[row, :128] = third[16 + row // 4] * 0.25
        back[64 + row, :128] = third[32 + row // 2] * 0.5
    spread = np.zeros((256, 384), np.float32)
    for tok in range(256):
        spread[tok, tok // 2] = 0.5
        spread[tok, 128 + tok // 4] = 0.25
        spread[tok, 192 + tok // 8] = 0.125
        spread[tok, 224 + tok // 8] = 0.125
        spread[tok, 256:384] = third[tok // 16] / 16
    return np.concatenate([pool, rise, back, spread], 0)


def flipped(place, k):
    if k == 0:
        return place
    if k == 1:
        return place + 1 - 2 * (place % 2)
    if k == 2:
        return place + 2 - 4 * (place // 2)
    return 3 - place


def nn(a, b):
    return lax.dot_general(a, b, (((1,), (0,)), ((), ())), preferred_element_type=F32)


def nt(a, b):
    return lax.dot_general(a, b, (((1,), (1,)), ((), ())), preferred_element_type=F32)


def tn(a, b):
    return lax.dot_general(a, b, (((0,), (0,)), ((), ())), preferred_element_type=F32)


SCRATCH = dict(
    xa=((4 * 256, D), BF),
    wv=((2, GROUPS, D, GC), BF),
    qv=((256, HALF), BF),
    gv=((256, HALF), BF),
    kl=((2, 192, HALF), BF),
    vl=((2, 192, HALF), BF),
    kt=((128, HALF), BF),
    vt=((128, HALF), BF),
    lo=((2, 64, HALF), BF),
    cc=((2, 256, HALF), BF),
    sp=((2, 2, 48, HALF), BF),
    sz=((2, 96, HALF), BF),
    dcb=((2, 256, HALF), BF),
    dcf=((2, 128, HALF), F32),
    rb=((2, 384, HALF), BF),
    sx=((2, 128, HALF), BF),
    ld=((2, 256, HALF), F32),
    gkv=((2, 256, HALF), BF),
    ao=((256, HALF), BF),
    qo=((256, HALF), BF),
    gs=((HALF, 256), BF),
    gt0=((192, 1024), BF),
    gt1=((64, 1024), BF),
    rs0=((2, 4, 4, 96, 128), BF),
    rs1=((2, 4, 4, 32, 128), BF),
    ra0=((2, 3, 4, 96, 128), BF),
    ra1=((2, 3, 4, 32, 128), BF),
    tf0=((2, 4, 96, 128), F32),
    tf1=((2, 4, 32, 128), F32),
    tb0=((2, 4, 96, 128), BF),
    tb1=((2, 4, 32, 128), BF),
    rz0=((2, 3, 96, 128), BF),
    rz1=((2, 3, 32, 128), BF),
    fo0=((192, 128), BF),
    fo1=((64, 128), BF),
    ow0=((2, 4, 192, 128), BF),
    ow1=((2, 4, 64, 128), BF),
    gxf=((128, D), F32),
    gxs=((128, D), BF),
    gxr=((128, D), BF),
    pp=((592, 384), BF),
)


def kernel(x_h, q_h, v_h, w_h, g_h, p_h, att_o, gx_o, gq_o, gv_o, gw_o, *rest):
    s = dict(zip(SCRATCH, rest[: len(SCRATCH)]))
    ssem, rsem = rest[len(SCRATCH) :]
    xa, wv, qv, gv, kl, vl, kt, vt, lo = (s[n] for n in ("xa", "wv", "qv", "gv", "kl", "vl", "kt", "vt", "lo"))
    cc, sp, sz, dcb, dcf, rb, sx, ld = (s[n] for n in ("cc", "sp", "sz", "dcb", "dcf", "rb", "sx", "ld"))
    gkv, ao, qo, gs = (s[n] for n in ("gkv", "ao", "qo", "gs"))
    gt, rs, ra, tf, tb, rz, fo, ow = ([s[n + p] for p in "01"] for n in ("gt", "rs", "ra", "tf", "tb", "rz", "fo", "ow"))
    gxf, gxs, gxr, pp = (s[n] for n in ("gxf", "gxs", "gxr", "pp"))

    y = lax.axis_index("dp")
    ctx = lax.axis_index("ctx")
    core = ctx % 2
    xx = (ctx // 2) % 4
    zz = ctx // 8
    mate = (y, ctx + 1 - 2 * core)
    along_x = [(y, zz * 8 + flipped(xx, k) * 2 + core) for k in range(4)]
    cross_x = [(y, zz * 8 + flipped(xx, k) * 2 + 1 - core) for k in range(4)]
    along_z = [(y, flipped(zz, k) * 8 + xx * 2 + core) for k in range(4)]
    along_y = [(flipped(y, k), ctx) for k in range(4)]
    cross_y = [(flipped(y, k), mate[1]) for k in range(4)]
    mine = pl.multiple_of(core * HALF, HALF)
    theirs = pl.multiple_of((1 - core) * HALF, HALF)

    peers = [mate] + along_x[1:] + cross_x[1:] + along_z[1:] + along_y[1:] + cross_y[1:]
    barrier = pltpu.get_barrier_semaphore()
    for peer in peers:
        pl.semaphore_signal(barrier, inc=1, device_id=peer, device_id_type=MESH)

    count = [0]
    arrivals = [0]
    sent = []
    stored = []

    class Landing:
        def __init__(self, whole, send_at):
            self.copy = pltpu.make_async_remote_copy(
                src_ref=whole,
                dst_ref=whole,
                send_sem=ssem.at[send_at],
                recv_sem=rsem.at[arrivals[0]],
                device_id=mate,
                device_id_type=MESH,
            )
            arrivals[0] += 1

    def start(src, dst, device, send_at, recv_at):
        pltpu.make_async_remote_copy(
            src_ref=src, dst_ref=dst, send_sem=ssem.at[send_at], recv_sem=rsem.at[recv_at], device_id=device, device_id_type=MESH
        ).start()

    class Route:
        def __init__(self, total):
            self.at = count[0]
            count[0] += 1
            sent.append((total, self.at))

        def send(self, whole, messages):
            landing = Landing(whole, self.at)
            for src, dst, device in messages:
                start(src, dst, device, self.at, arrivals[0] - 1)
            return landing

    def remote(src, dst, device):
        return Route(dst).send(dst, [(src, dst, device)])

    def local(src, dst):
        at = count[0]
        count[0] += 1
        copy = pltpu.make_async_copy(src, dst, ssem.at[at])
        copy.start()
        return copy

    def arrive(copies):
        for copy in copies:
            copy.copy.wait_recv()

    def cols(j):
        return pl.ds(j * GC, GC)

    def head_cols(i):
        return pl.ds(i * DH, DH)

    in_x = local(x_h, xa.at[0:128])
    in_p = local(p_h, pp)
    in_v = [local(v_h.at[:, pl.ds(mine, HALF)], vl.at[0, 0:128]), local(v_h.at[:, pl.ds(theirs, HALF)], vt)]
    in_w = [
        [local(w_h.at[:, pl.ds(pl.multiple_of(side + j * GC, GC), GC)], wv.at[h, j]) for h, side in enumerate((mine, theirs))]
        for j in range(GROUPS)
    ]
    in_q = local(q_h.at[:, pl.ds(mine, HALF)], qv.at[0:128])
    in_g = local(g_h.at[:, pl.ds(mine, HALF)], gv.at[0:128])

    def pooled(kv, ref, h, j, rows_in):
        rows = nn(pp[0:112, 0:128], rows_in).astype(BF)
        sp[h, kv, :, cols(j)] = rows[64:112]
        if h == 0:
            ref[1, 128:192, cols(j)] = rows[0:64]
            lo[kv, 0:32, cols(j)] = rows[64:96]

    in_p.wait()
    for copy in in_v:
        copy.wait()
    for j in range(GROUPS):
        pooled(1, vl, 0, j, vl[0, 0:128, cols(j)])
        pooled(1, vl, 1, j, vt[:, cols(j)])
    in_x.wait()
    for j in range(GROUPS):
        for h in (0, 1):
            in_w[j][h].wait()
            keys = nn(xa[0:128, :], wv[h, j]).astype(BF)
            if h == 0:
                kl[0, 0:128, cols(j)] = keys
            else:
                kt[:, cols(j)] = keys
            pooled(0, kl, h, j, keys)

    pl.semaphore_wait(barrier, len(peers))
    fx_route, fz_route = Route(cc.at[:, 0:128]), Route(cc.at[:, 128:256])
    bx_route, bz_route = Route(rb.at[:, 128:256]), Route(rb.at[:, 256:384])

    def send_x(i):
        at = head_cols(i)
        messages = []
        for h, line in ((0, along_x), (1, cross_x)):
            first = sp.at[h, :, 0:32, at]
            second = sp.at[h, :, 32:48, at]
            messages.append((first, cc.at[:, 32 * h : 32 * h + 32, at], line[1]))
            messages.append((second, cc.at[:, 64 + 16 * h : 80 + 16 * h, at], line[2]))
            messages.append((second, cc.at[:, 96 + 16 * h : 112 + 16 * h, at], line[3]))
        return fx_route.send(cc.at[:, 0:128, at], messages)

    fx = [send_x(0)]
    m_k = remote(kt, kl.at[1, 0:128], mate)
    m_v = remote(vt, vl.at[1, 0:128], mate)
    for i in range(1, HEADS):
        fx.append(send_x(i))
    y_x = {k: remote(x_h, xa.at[k * 256 : k * 256 + 128], along_y[k]) for k in (1, 3)}
    m_q = remote(q_h.at[:, pl.ds(theirs, HALF)], qv.at[128:256], mate)
    m_g = remote(g_h.at[:, pl.ds(theirs, HALF)], gv.at[128:256], mate)
    m_x = remote(x_h, xa.at[128:256], mate)

    arrive([m_k, m_v])
    for kv, ref in ((0, kl), (1, vl)):
        for j in range(GROUPS):
            rows = nn(pp[0:96, 0:128], ref[1, 0:128, cols(j)]).astype(BF)
            ref[0, 128:192, cols(j)] = rows[0:64]
            lo[kv, 32:64, cols(j)] = rows[64:96]

    def rise(i):
        arrive([fx[i]])
        at = head_cols(i)
        for kv in (0, 1):
            rows = nn(pp[112:208, 0:64], lo[kv, :, at]) + nn(pp[112:208, 128:256], cc[kv, 0:128, at])
            sz[kv, :, at] = rows.astype(BF)
        return fz_route.send(
            cc.at[:, 128:256, at],
            [
                (sz.at[:, 0:64, at], cc.at[:, 128:192, at], along_z[1]),
                (sz.at[:, 64:96, at], cc.at[:, 192:224, at], along_z[2]),
                (sz.at[:, 64:96, at], cc.at[:, 224:256, at], along_z[3]),
            ],
        )

    def head(c):
        q = qv[:, c]
        g = gv[:, c]
        ck = cc[0, :, c]
        cv = cc[1, :, c]
        rate = SCALE * math.log2(math.e)
        e1 = jnp.exp2(nt(q, ck) * rate)
        total = jnp.sum(e1, -1, keepdims=True)
        pair = [slice(0, 128), slice(128, 256)]
        e0 = [jnp.exp2(nt(q[pair[b]], kl[b, :, c]) * rate) for b in (0, 1)]
        total = total + jnp.concatenate([jnp.sum(e, -1, keepdims=True) for e in e0], 0)
        inverse = 1.0 / (total * 0.25)
        p1 = e1 * inverse
        p0 = [e0[b] * inverse[pair[b]] for b in (0, 1)]
        p1b = p1.astype(BF)
        p0b = [p.astype(BF) for p in p0]
        out = (nn(p1b, cv) + jnp.concatenate([nn(p0b[b], vl[b, :, c]) for b in (0, 1)], 0)) * 0.25
        ao[:, c] = out.astype(BF)
        delta = jnp.sum(g.astype(F32) * out, -1, keepdims=True)
        d1 = (p1 * (nt(g, cv) - delta)).astype(BF)
        d0 = [(p0[b] * (nt(g[pair[b]], vl[b, :, c]) - delta[pair[b]])).astype(BF) for b in (0, 1)]
        fold = SCALE * 0.25
        dq = (nn(d1, ck) + jnp.concatenate([nn(d0[b], kl[b, :, c]) for b in (0, 1)], 0)) * fold
        qo[:, c] = dq.astype(BF)
        dck = tn(d1, q) * fold
        dcv = tn(p1b, g) * 0.25
        dcf[0, :, c] = dck[0:128]
        dcf[1, :, c] = dcv[0:128]
        dcb[0, 128:256, c] = dck[128:256].astype(BF)
        dcb[1, 128:256, c] = dcv[128:256].astype(BF)
        for b in (0, 1):
            dk = tn(d0[b], q[pair[b]]) * fold
            dv = tn(p0b[b], g[pair[b]]) * 0.25
            ld[0, pair[b], c] = dk[0:128]
            ld[1, pair[b], c] = dv[0:128]
            other = slice(64 - 64 * b, 128 - 64 * b)
            rb[0, other, c] = dk[128:192].astype(BF)
            rb[1, other, c] = dv[128:192].astype(BF)

    def attend(i, landing):
        arrive([landing])
        at = head_cols(i)
        head(at)
        return bz_route.send(
            rb.at[:, 256:384, at],
            [
                (dcb.at[:, 128:192, at], rb.at[:, 256:320, at], along_z[1]),
                (dcb.at[:, 192:224, at], rb.at[:, 320:352, at], along_z[2]),
                (dcb.at[:, 224:256, at], rb.at[:, 352:384, at], along_z[3]),
            ],
        )

    def return_x(i, landing):
        arrive([landing])
        at = head_cols(i)
        for kv in (0, 1):
            sx[kv, :, at] = (dcf[kv, :, at] + nn(pp[208:336, 0:128], rb[kv, 256:384, at])).astype(BF)
        return bx_route.send(
            rb.at[:, 128:256, at],
            [
                (sx.at[:, 0:64, at], rb.at[:, 128:192, at], along_x[1]),
                (sx.at[:, 64:96, at], rb.at[:, 192:224, at], along_x[2]),
                (sx.at[:, 96:128, at], rb.at[:, 224:256, at], along_x[3]),
            ],
        )

    def finish(i, landing):
        arrive([landing])
        at = head_cols(i)
        for kv in (0, 1):
            total = ld[kv, :, at] + nn(pp[336:592, :], rb[kv, :, at])
            gkv[kv, :, at] = total.astype(BF)
            if kv == 0:
                gs[at, :] = total.T.astype(BF)

    def send_y(p):
        first, last = PARTS[p]
        each = (last - first) * 32
        quarter = [pl.ds(pl.multiple_of(first * DH + flipped(y, k) * each, 64), each) for k in range(4)]
        landing = Route(gt[p].at[:, 256:1024]).send(
            gt[p].at[:, 256:1024],
            [(gs.at[quarter[k]], gt[p].at[:, k * 256 : (k + 1) * 256], along_y[k]) for k in (1, 2, 3)],
        )
        gt[p][:, 0:256] = gs[quarter[0], :]
        return landing

    def forward(k):
        arrive([y_x[k]])
        rows = 0 if k == 1 else 64
        ahead = remote(xa.at[k * 256 + rows : k * 256 + rows + 64], xa.at[512 + rows : 512 + rows + 64], along_y[4 - k])
        return remote(xa.at[k * 256 : k * 256 + 128], xa.at[k * 256 + 128 : k * 256 + 256], mate), ahead

    lines = ((xx, along_x), (zz, along_z))

    def weights(p, landing):
        arrive([landing])
        each = rs[p].shape[3]

        def step(i, carry):
            part = nn(gt[p][...], xa[:, pl.ds(pl.multiple_of(i * 256, 256), 256)]).astype(BF)
            z_at = i // 2
            x_at = 2 * (i % 2)
            for n in (0, 1):
                rs[p][0, x_at + n, z_at] = part[0:each, n * 128 : n * 128 + 128]
                rs[p][1, z_at, x_at + n] = part[each : 2 * each, n * 128 : n * 128 + 128]
            return carry

        lax.fori_loop(0, 8, step, 0)
        return Route(ra[p]).send(
            ra[p],
            [
                (rs[p].at[d, flipped(lines[d][0], k)], ra[p].at[d, k - 1], lines[d][1][k])
                for k in (2, 1, 3)
                for d in (0, 1)
            ],
        )

    def second(p, landing):
        arrive([landing])
        messages = []
        for d in (0, 1):
            total = rs[p][d, lines[d][0]].astype(F32)
            for k in range(3):
                total = total + ra[p][d, k].astype(F32)
            tf[p][d] = total
            tb[p][d] = total.astype(BF)
            place, line = lines[1 - d]
            messages += [(tb[p].at[d, flipped(place, k)], rz[p].at[d, k - 1], line[k]) for k in (2, 1, 3)]
        return Route(rz[p]).send(rz[p], messages)

    def third(p, landing):
        arrive([landing])
        each = rs[p].shape[3]
        for d in (0, 1):
            total = tf[p][d, lines[1 - d][0]]
            for k in range(3):
                total = total + rz[p][d, k].astype(F32)
            fo[p][d * each : d * each + each] = total.astype(BF)
        whole = xa.at[0 : 7 * each, 0:256]
        landing = Route(whole).send(
            whole,
            [(fo[p], ow[p].at[core, y], along_y[k]) for k in (2, 1, 3)]
            + [(fo[p], ow[p].at[core, y], cross_y[k]) for k in (2, 1, 3, 0)],
        )
        ow[p][core, y] = fo[p][...]
        return landing

    def assemble(p, landing):
        arrive([landing])
        first, last = PARTS[p]
        wide = (last - first) * DH
        for side in (0, 1):
            turned = ow[p][side].astype(F32).reshape(wide, 128).T
            gw_o[:, pl.ds(side * HALF + first * DH, wide)] = jnp.where(core == 0, turned[0:64], turned[64:128])

    def give(staged, out):
        stored.append(local(staged.at[0:128], out.at[:, pl.ds(mine, HALF)]))
        return remote(staged.at[128:256], out.at[:, pl.ds(mine, HALF)], mate)

    def partial(i, carry):
        at = pl.ds(pl.multiple_of(i * 256, 256), 256)
        total = nt(gkv[0, :, cols(0)], wv[0, 0, at, :])
        for j in range(1, GROUPS):
            total = total + nt(gkv[0, :, cols(j)], wv[0, j, at, :])
        gxf[:, at] = total[0:128]
        gxs[:, at] = total[128:256].astype(BF)
        return carry

    fz = [rise(i) for i in range(4)]
    in_q.wait()
    in_g.wait()
    arrive([m_q, m_g])
    bz, bx = [], []
    for i in range(4):
        bz.append(attend(i, fz[i]))
        fz.append(rise(4 + i))
    f1, a1 = forward(1)
    f3, a3 = forward(3)
    bz.append(attend(4, fz[4]))
    bz.append(attend(5, fz[5]))
    bx.append(return_x(0, bz[0]))
    bx.append(return_x(1, bz[1]))
    bz.append(attend(6, fz[6]))
    bx.append(return_x(2, bz[2]))
    bz.append(attend(7, fz[7]))
    given = [give(ao, att_o), give(qo, gq_o)]
    bx.append(return_x(3, bz[3]))
    bx.append(return_x(4, bz[4]))
    finish(0, bx[0])
    bx.append(return_x(5, bz[5]))
    finish(1, bx[1])
    bx.append(return_x(6, bz[6]))
    finish(2, bx[2])
    bx.append(return_x(7, bz[7]))
    arrive([a1, a3])
    f2 = remote(xa.at[512:640], xa.at[640:768], mate)
    finish(3, bx[3])
    finish(4, bx[4])
    finish(5, bx[5])
    gy0 = send_y(0)
    finish(6, bx[6])
    finish(7, bx[7])
    gy1 = send_y(1)
    given.append(give(gkv.at[1], gv_o))
    arrive([m_x, f1, f3, f2])
    wa0 = weights(0, gy0)
    wa1 = weights(1, gy1)
    wb0 = second(0, wa0)
    lax.fori_loop(0, 8, partial, 0)
    gxc = remote(gxs, gxr, mate)
    wb1 = second(1, wa1)
    wc0 = third(0, wb0)
    wc1 = third(1, wb1)
    arrive([gxc])
    gx_o[...] = (gxf[...] + gxr[...].astype(F32)).astype(BF)
    assemble(0, wc0)
    assemble(1, wc1)
    arrive(given)
    assert count[0] <= SENDS and arrivals[0] <= LANDINGS, (count, arrivals)
    for copy in stored:
        copy.wait()
    for total, at in sent:
        pltpu.make_async_remote_copy(
            src_ref=total, dst_ref=total, send_sem=ssem.at[at], recv_sem=rsem.at[0], device_id=mate, device_id_type=MESH
        ).wait_send()


def hand_over(*refs):
    sources, outs, sem = refs[:5], refs[5:10], refs[10]
    copies = [pltpu.make_async_copy(src, out, sem.at[i]) for i, (src, out) in enumerate(zip(sources, outs))]
    for copy in copies:
        copy.start()
    for copy in copies:
        copy.wait()


def body(tokens, queries, values, key_weight, grad_out):
    anywhere = pl.BlockSpec(memory_space=pl.ANY)
    block = jax.ShapeDtypeStruct((TOK, D), BF)
    shapes = [block] * 4 + [jax.ShapeDtypeStruct((64, D), F32)]
    held = [pltpu.VMEM(shape.shape, shape.dtype) for shape in shapes]
    results = pl.pallas_call(
        kernel,
        out_shape=held,
        in_specs=[anywhere] * 6,
        out_specs=[pl.BlockSpec(memory_space=pltpu.VMEM)] * 5,
        scratch_shapes=[pltpu.VMEM(shape, dtype) for shape, dtype in SCRATCH.values()]
        + [pltpu.SemaphoreType.DMA((SENDS,)), pltpu.SemaphoreType.DMA((LANDINGS,))],
        compiler_params=pltpu.CompilerParams(
            collective_id=0, has_side_effects=True, vmem_limit_bytes=56 * 1024 * 1024
        ),
        name="hierarchical_attention",
    )(tokens[0], queries[0], values[0], key_weight, grad_out[0], jnp.asarray(matrices(), BF))
    att, gx, gq, gv, gw = pl.pallas_call(
        hand_over,
        out_shape=shapes,
        in_specs=[pl.BlockSpec(memory_space=pltpu.VMEM)] * 5,
        out_specs=[anywhere] * 5,
        scratch_shapes=[pltpu.SemaphoreType.DMA((5,))],
        name="hand_over",
    )(*[pltpu.with_memory_space_constraint(r, pltpu.VMEM) for r in results])
    return att[None], gx[None], gq[None], gv[None], gw


def solution(mesh):
    split = P("dp", "ctx", None)
    return jax.shard_map(
        body,
        mesh=mesh,
        in_specs=(split, split, split, P(), split),
        out_specs=(split, split, split, split, P("ctx", None)),
        check_vma=False,
    )
```

```python
import math

import jax
import jax.numpy as jnp
import numpy as np
from jax import lax
from jax.experimental import pallas as pl
from jax.experimental.pallas import tpu as pltpu
from jax.sharding import PartitionSpec as P

DH = 128
TOK = 128
D = 2048
HALF = D // 2
GROUPS = 4
GC = HALF // GROUPS
HEADS = 8
PARTS = ((0, 4), (4, 7), (7, 8))
SCALE = DH ** (-0.5)
BF = jnp.bfloat16
F32 = jnp.float32
MESH = pl.DeviceIdType.MESH
SENDS = 52
LANDINGS = 60


def matrices():
    pool = np.zeros((112, 384), np.float32)
    for tok in range(128):
        pool[tok // 2, tok] = 0.5
        pool[64 + tok // 4, tok] = 0.25
        pool[96 + tok // 8, tok] = 0.125
    rise = np.zeros((96, 384), np.float32)
    for row in range(64):
        rise[row // 4, row] = 0.25
        rise[64 + row // 8, row] = 0.125
        rise[16 + row // 4, 128 + row] = 0.25
        rise[72 + row // 8, 128 + row] = 0.125
        rise[32 + row // 2, 192 + row] = 0.5
        rise[80 + row // 4, 192 + row] = 0.25
    third = np.zeros((64, 128), np.float32)
    for row in range(64):
        third[row, row] = 1.0
        third[row, 64 + row // 2] = 0.5
        third[row, 96 + row // 2] = 0.5
    back = np.zeros((128, 384), np.float32)
    for row in range(64):
        back[row, :128] = third[16 + row // 4] * 0.25
        back[64 + row, :128] = third[32 + row // 2] * 0.5
    spread = np.zeros((256, 384), np.float32)
    for tok in range(256):
        spread[tok, tok // 2] = 0.5
        spread[tok, 128 + tok // 4] = 0.25
        spread[tok, 192 + tok // 8] = 0.125
        spread[tok, 224 + tok // 8] = 0.125
        spread[tok, 256:384] = third[tok // 16] / 16
    return np.concatenate([pool, rise, back, spread], 0)


def flipped(place, k):
    if k == 0:
        return place
    if k == 1:
        return place + 1 - 2 * (place % 2)
    if k == 2:
        return place + 2 - 4 * (place // 2)
    return 3 - place


def nn(a, b):
    return lax.dot_general(a, b, (((1,), (0,)), ((), ())), preferred_element_type=F32)


def nt(a, b):
    return lax.dot_general(a, b, (((1,), (1,)), ((), ())), preferred_element_type=F32)


def tn(a, b):
    return lax.dot_general(a, b, (((0,), (0,)), ((), ())), preferred_element_type=F32)


SCRATCH = dict(
    xa=((4 * 256, D), BF),
    wv=((2, GROUPS, D, GC), BF),
    qv=((256, HALF), BF),
    gv=((256, HALF), BF),
    kl=((2, 192, HALF), BF),
    vl=((2, 192, HALF), BF),
    kt=((128, HALF), BF),
    vt=((128, HALF), BF),
    lo=((2, 64, HALF), BF),
    cc=((2, 256, HALF), BF),
    sp=((2, 2, 48, HALF), BF),
    sz=((2, 96, HALF), BF),
    dcb=((2, 256, HALF), BF),
    dcf=((2, 128, HALF), F32),
    rb=((2, 384, HALF), BF),
    sx=((2, 128, HALF), BF),
    ld=((2, 256, HALF), F32),
    gkv=((2, 256, HALF), BF),
    ao=((256, HALF), BF),
    qo=((256, HALF), BF),
    gs=((HALF, 256), BF),
    gt0=((128, 1024), BF),
    gt1=((96, 1024), BF),
    gt2=((32, 1024), BF),
    rs0=((2, 4, 4, 64, 128), BF),
    rs1=((2, 4, 4, 48, 128), BF),
    rs2=((2, 4, 4, 16, 128), BF),
    ra0=((2, 3, 4, 64, 128), BF),
    ra1=((2, 3, 4, 48, 128), BF),
    ra2=((2, 3, 4, 16, 128), BF),
    tf0=((2, 4, 64, 128), F32),
    tf1=((2, 4, 48, 128), F32),
    tf2=((2, 4, 16, 128), F32),
    tb0=((2, 4, 64, 128), BF),
    tb1=((2, 4, 48, 128), BF),
    tb2=((2, 4, 16, 128), BF),
    rz0=((2, 3, 64, 128), BF),
    rz1=((2, 3, 48, 128), BF),
    rz2=((2, 3, 16, 128), BF),
    fo0=((128, 128), BF),
    fo1=((96, 128), BF),
    fo2=((32, 128), BF),
    ow0=((2, 4, 128, 128), BF),
    ow1=((2, 4, 96, 128), BF),
    ow2=((2, 4, 32, 128), BF),
    gxf=((128, D), F32),
    gxs=((128, D), BF),
    gxr=((128, D), BF),
    pp=((592, 384), BF),
)


def kernel(x_h, q_h, v_h, w_h, g_h, p_h, att_o, gx_o, gq_o, gv_o, gw_o, *rest):
    s = dict(zip(SCRATCH, rest[: len(SCRATCH)]))
    ssem, rsem = rest[len(SCRATCH) :]
    xa, wv, qv, gv, kl, vl, kt, vt, lo = (s[n] for n in ("xa", "wv", "qv", "gv", "kl", "vl", "kt", "vt", "lo"))
    cc, sp, sz, dcb, dcf, rb, sx, ld = (s[n] for n in ("cc", "sp", "sz", "dcb", "dcf", "rb", "sx", "ld"))
    gkv, ao, qo, gs = (s[n] for n in ("gkv", "ao", "qo", "gs"))
    gt, rs, ra, tf, tb, rz, fo, ow = ([s[n + p] for p in "012"] for n in ("gt", "rs", "ra", "tf", "tb", "rz", "fo", "ow"))
    gxf, gxs, gxr, pp = (s[n] for n in ("gxf", "gxs", "gxr", "pp"))

    y = lax.axis_index("dp")
    ctx = lax.axis_index("ctx")
    core = ctx % 2
    xx = (ctx // 2) % 4
    zz = ctx // 8
    mate = (y, ctx + 1 - 2 * core)
    along_x = [(y, zz * 8 + flipped(xx, k) * 2 + core) for k in range(4)]
    cross_x = [(y, zz * 8 + flipped(xx, k) * 2 + 1 - core) for k in range(4)]
    along_z = [(y, flipped(zz, k) * 8 + xx * 2 + core) for k in range(4)]
    along_y = [(flipped(y, k), ctx) for k in range(4)]
    cross_y = [(flipped(y, k), mate[1]) for k in range(4)]
    mine = pl.multiple_of(core * HALF, HALF)
    theirs = pl.multiple_of((1 - core) * HALF, HALF)

    peers = [mate] + along_x[1:] + cross_x[1:] + along_z[1:] + along_y[1:] + cross_y[1:]
    barrier = pltpu.get_barrier_semaphore()
    for peer in peers:
        pl.semaphore_signal(barrier, inc=1, device_id=peer, device_id_type=MESH)

    count = [0]
    arrivals = [0]
    sent = []
    stored = []

    class Landing:
        def __init__(self, whole, send_at):
            self.copy = pltpu.make_async_remote_copy(
                src_ref=whole,
                dst_ref=whole,
                send_sem=ssem.at[send_at],
                recv_sem=rsem.at[arrivals[0]],
                device_id=mate,
                device_id_type=MESH,
            )
            arrivals[0] += 1

    def start(src, dst, device, send_at, recv_at):
        pltpu.make_async_remote_copy(
            src_ref=src, dst_ref=dst, send_sem=ssem.at[send_at], recv_sem=rsem.at[recv_at], device_id=device, device_id_type=MESH
        ).start()

    class Route:
        def __init__(self, total):
            self.at = count[0]
            count[0] += 1
            sent.append((total, self.at))

        def send(self, whole, messages):
            landing = Landing(whole, self.at)
            for src, dst, device in messages:
                start(src, dst, device, self.at, arrivals[0] - 1)
            return landing

    def remote(src, dst, device):
        return Route(dst).send(dst, [(src, dst, device)])

    def local(src, dst):
        at = count[0]
        count[0] += 1
        copy = pltpu.make_async_copy(src, dst, ssem.at[at])
        copy.start()
        return copy

    def arrive(copies):
        for copy in copies:
            copy.copy.wait_recv()

    def cols(j):
        return pl.ds(j * GC, GC)

    def head_cols(i):
        return pl.ds(i * DH, DH)

    in_x = local(x_h, xa.at[0:128])
    in_p = local(p_h, pp)
    in_v = [local(v_h.at[:, pl.ds(mine, HALF)], vl.at[0, 0:128]), local(v_h.at[:, pl.ds(theirs, HALF)], vt)]
    in_w = [
        [local(w_h.at[:, pl.ds(pl.multiple_of(side + j * GC, GC), GC)], wv.at[h, j]) for h, side in enumerate((mine, theirs))]
        for j in range(GROUPS)
    ]
    in_q = local(q_h.at[:, pl.ds(mine, HALF)], qv.at[0:128])
    in_g = local(g_h.at[:, pl.ds(mine, HALF)], gv.at[0:128])

    def pooled(kv, ref, h, j, rows_in):
        rows = nn(pp[0:112, 0:128], rows_in).astype(BF)
        sp[h, kv, :, cols(j)] = rows[64:112]
        if h == 0:
            ref[1, 128:192, cols(j)] = rows[0:64]
            lo[kv, 0:32, cols(j)] = rows[64:96]

    in_p.wait()
    for copy in in_v:
        copy.wait()
    for j in range(GROUPS):
        pooled(1, vl, 0, j, vl[0, 0:128, cols(j)])
        pooled(1, vl, 1, j, vt[:, cols(j)])
    in_x.wait()
    for j in range(GROUPS):
        for h in (0, 1):
            in_w[j][h].wait()
            keys = nn(xa[0:128, :], wv[h, j]).astype(BF)
            if h == 0:
                kl[0, 0:128, cols(j)] = keys
            else:
                kt[:, cols(j)] = keys
            pooled(0, kl, h, j, keys)

    pl.semaphore_wait(barrier, len(peers))
    fx_route, fz_route = Route(cc.at[:, 0:128]), Route(cc.at[:, 128:256])
    bx_route, bz_route = Route(rb.at[:, 128:256]), Route(rb.at[:, 256:384])

    def send_x(i):
        at = head_cols(i)
        messages = []
        for h, line in ((0, along_x), (1, cross_x)):
            first = sp.at[h, :, 0:32, at]
            second = sp.at[h, :, 32:48, at]
            messages.append((first, cc.at[:, 32 * h : 32 * h + 32, at], line[1]))
            messages.append((second, cc.at[:, 64 + 16 * h : 80 + 16 * h, at], line[2]))
            messages.append((second, cc.at[:, 96 + 16 * h : 112 + 16 * h, at], line[3]))
        return fx_route.send(cc.at[:, 0:128, at], messages)

    fx = [send_x(0)]
    m_k = remote(kt, kl.at[1, 0:128], mate)
    m_v = remote(vt, vl.at[1, 0:128], mate)
    for i in range(1, HEADS):
        fx.append(send_x(i))
    y_x = {k: remote(x_h, xa.at[k * 256 : k * 256 + 128], along_y[k]) for k in (1, 3)}
    m_q = remote(q_h.at[:, pl.ds(theirs, HALF)], qv.at[128:256], mate)
    m_g = remote(g_h.at[:, pl.ds(theirs, HALF)], gv.at[128:256], mate)
    m_x = remote(x_h, xa.at[128:256], mate)

    arrive([m_k, m_v])
    for kv, ref in ((0, kl), (1, vl)):
        for j in range(GROUPS):
            rows = nn(pp[0:96, 0:128], ref[1, 0:128, cols(j)]).astype(BF)
            ref[0, 128:192, cols(j)] = rows[0:64]
            lo[kv, 32:64, cols(j)] = rows[64:96]

    def rise(i):
        arrive([fx[i]])
        at = head_cols(i)
        for kv in (0, 1):
            rows = nn(pp[112:208, 0:64], lo[kv, :, at]) + nn(pp[112:208, 128:256], cc[kv, 0:128, at])
            sz[kv, :, at] = rows.astype(BF)
        return fz_route.send(
            cc.at[:, 128:256, at],
            [
                (sz.at[:, 0:64, at], cc.at[:, 128:192, at], along_z[1]),
                (sz.at[:, 64:96, at], cc.at[:, 192:224, at], along_z[2]),
                (sz.at[:, 64:96, at], cc.at[:, 224:256, at], along_z[3]),
            ],
        )

    def head(c):
        q = qv[:, c]
        g = gv[:, c]
        ck = cc[0, :, c]
        cv = cc[1, :, c]
        rate = SCALE * math.log2(math.e)
        e1 = jnp.exp2(nt(q, ck) * rate)
        total = jnp.sum(e1, -1, keepdims=True)
        pair = [slice(0, 128), slice(128, 256)]
        e0 = [jnp.exp2(nt(q[pair[b]], kl[b, :, c]) * rate) for b in (0, 1)]
        total = total + jnp.concatenate([jnp.sum(e, -1, keepdims=True) for e in e0], 0)
        inverse = 1.0 / (total * 0.25)
        p1 = e1 * inverse
        p0 = [e0[b] * inverse[pair[b]] for b in (0, 1)]
        p1b = p1.astype(BF)
        p0b = [p.astype(BF) for p in p0]
        out = (nn(p1b, cv) + jnp.concatenate([nn(p0b[b], vl[b, :, c]) for b in (0, 1)], 0)) * 0.25
        ao[:, c] = out.astype(BF)
        delta = jnp.sum(g.astype(F32) * out, -1, keepdims=True)
        d1 = (p1 * (nt(g, cv) - delta)).astype(BF)
        d0 = [(p0[b] * (nt(g[pair[b]], vl[b, :, c]) - delta[pair[b]])).astype(BF) for b in (0, 1)]
        fold = SCALE * 0.25
        dq = (nn(d1, ck) + jnp.concatenate([nn(d0[b], kl[b, :, c]) for b in (0, 1)], 0)) * fold
        qo[:, c] = dq.astype(BF)
        dck = tn(d1, q) * fold
        dcv = tn(p1b, g) * 0.25
        dcf[0, :, c] = dck[0:128]
        dcf[1, :, c] = dcv[0:128]
        dcb[0, 128:256, c] = dck[128:256].astype(BF)
        dcb[1, 128:256, c] = dcv[128:256].astype(BF)
        for b in (0, 1):
            dk = tn(d0[b], q[pair[b]]) * fold
            dv = tn(p0b[b], g[pair[b]]) * 0.25
            ld[0, pair[b], c] = dk[0:128]
            ld[1, pair[b], c] = dv[0:128]
            other = slice(64 - 64 * b, 128 - 64 * b)
            rb[0, other, c] = dk[128:192].astype(BF)
            rb[1, other, c] = dv[128:192].astype(BF)

    def attend(i, landing):
        arrive([landing])
        at = head_cols(i)
        head(at)
        return bz_route.send(
            rb.at[:, 256:384, at],
            [
                (dcb.at[:, 128:192, at], rb.at[:, 256:320, at], along_z[1]),
                (dcb.at[:, 192:224, at], rb.at[:, 320:352, at], along_z[2]),
                (dcb.at[:, 224:256, at], rb.at[:, 352:384, at], along_z[3]),
            ],
        )

    def return_x(i, landing):
        arrive([landing])
        at = head_cols(i)
        for kv in (0, 1):
            sx[kv, :, at] = (dcf[kv, :, at] + nn(pp[208:336, 0:128], rb[kv, 256:384, at])).astype(BF)
        return bx_route.send(
            rb.at[:, 128:256, at],
            [
                (sx.at[:, 0:64, at], rb.at[:, 128:192, at], along_x[1]),
                (sx.at[:, 64:96, at], rb.at[:, 192:224, at], along_x[2]),
                (sx.at[:, 96:128, at], rb.at[:, 224:256, at], along_x[3]),
            ],
        )

    def finish(i, landing):
        arrive([landing])
        at = head_cols(i)
        for kv in (0, 1):
            total = ld[kv, :, at] + nn(pp[336:592, :], rb[kv, :, at])
            gkv[kv, :, at] = total.astype(BF)
            if kv == 0:
                gs[at, :] = total.T.astype(BF)

    def send_y(p):
        first, last = PARTS[p]
        each = (last - first) * 32
        quarter = [pl.ds(pl.multiple_of(first * DH + flipped(y, k) * each, 32), each) for k in range(4)]
        landing = Route(gt[p].at[:, 256:1024]).send(
            gt[p].at[:, 256:1024],
            [(gs.at[quarter[k]], gt[p].at[:, k * 256 : (k + 1) * 256], along_y[k]) for k in (1, 2, 3)],
        )
        gt[p][:, 0:256] = gs[quarter[0], :]
        return landing

    def forward(k):
        arrive([y_x[k]])
        rows = 0 if k == 1 else 64
        ahead = remote(xa.at[k * 256 + rows : k * 256 + rows + 64], xa.at[512 + rows : 512 + rows + 64], along_y[4 - k])
        return remote(xa.at[k * 256 : k * 256 + 128], xa.at[k * 256 + 128 : k * 256 + 256], mate), ahead

    lines = ((xx, along_x), (zz, along_z))

    def weights(p, landing):
        arrive([landing])
        each = rs[p].shape[3]

        columns = gt[p][...]
        for i in range(8):
            part = nn(columns, xa[:, i * 256 : i * 256 + 256]).astype(BF)
            for n in (0, 1):
                x_at = 2 * (i % 2) + n
                rs[p][0, x_at, i // 2] = part[0:each, n * 128 : n * 128 + 128]
                rs[p][1, i // 2, x_at] = part[each : 2 * each, n * 128 : n * 128 + 128]
        return Route(ra[p]).send(
            ra[p],
            [
                (rs[p].at[d, flipped(lines[d][0], k)], ra[p].at[d, k - 1], lines[d][1][k])
                for k in (2, 1, 3)
                for d in (0, 1)
            ],
        )

    def second(p, landing):
        arrive([landing])
        messages = []
        for d in (0, 1):
            total = rs[p][d, lines[d][0]].astype(F32)
            for k in range(3):
                total = total + ra[p][d, k].astype(F32)
            tf[p][d] = total
            tb[p][d] = total.astype(BF)
            place, line = lines[1 - d]
            messages += [(tb[p].at[d, flipped(place, k)], rz[p].at[d, k - 1], line[k]) for k in (2, 1, 3)]
        return Route(rz[p]).send(rz[p], messages)

    def third(p, landing):
        arrive([landing])
        each = rs[p].shape[3]
        for d in (0, 1):
            total = tf[p][d, lines[1 - d][0]]
            for k in range(3):
                total = total + rz[p][d, k].astype(F32)
            fo[p][d * each : d * each + each] = total.astype(BF)
        whole = xa.at[0 : 7 * each, 0:256]
        landing = Route(whole).send(
            whole,
            [(fo[p], ow[p].at[core, y], along_y[k]) for k in (2, 1, 3)]
            + [(fo[p], ow[p].at[core, y], cross_y[k]) for k in (2, 1, 3, 0)],
        )
        ow[p][core, y] = fo[p][...]
        return landing

    def assemble(p, landing):
        arrive([landing])
        first, last = PARTS[p]
        wide = (last - first) * DH
        for side in (0, 1):
            turned = ow[p][side].astype(F32).reshape(wide, 128).T
            gw_o[:, pl.ds(side * HALF + first * DH, wide)] = jnp.where(core == 0, turned[0:64], turned[64:128])

    def give(staged, out):
        stored.append(local(staged.at[0:128], out.at[:, pl.ds(mine, HALF)]))
        return remote(staged.at[128:256], out.at[:, pl.ds(mine, HALF)], mate)

    def partial():
        for i in range(8):
            at = pl.ds(i * 256, 256)
            total = nt(gkv[0, :, cols(0)], wv[0, 0, at, :])
            for j in range(1, GROUPS):
                total = total + nt(gkv[0, :, cols(j)], wv[0, j, at, :])
            gxf[:, at] = total[0:128]
            gxs[:, at] = total[128:256].astype(BF)

    fz = [rise(i) for i in range(8)]
    in_q.wait()
    in_g.wait()
    arrive([m_q, m_g])
    bz, bx = [], []
    for i in range(4):
        bz.append(attend(i, fz[i]))
    f1, a1 = forward(1)
    f3, a3 = forward(3)
    bz.append(attend(4, fz[4]))
    bx.append(return_x(0, bz[0]))
    bz.append(attend(5, fz[5]))
    bx.append(return_x(1, bz[1]))
    bz.append(attend(6, fz[6]))
    bx.append(return_x(2, bz[2]))
    bz.append(attend(7, fz[7]))
    given = [give(ao, att_o), give(qo, gq_o)]
    bx.append(return_x(3, bz[3]))
    finish(0, bx[0])
    bx.append(return_x(4, bz[4]))
    finish(1, bx[1])
    bx.append(return_x(5, bz[5]))
    finish(2, bx[2])
    bx.append(return_x(6, bz[6]))
    finish(3, bx[3])
    gy0 = send_y(0)
    bx.append(return_x(7, bz[7]))
    arrive([a1, a3])
    f2 = remote(xa.at[512:640], xa.at[640:768], mate)
    finish(4, bx[4])
    finish(5, bx[5])
    finish(6, bx[6])
    gy1 = send_y(1)
    finish(7, bx[7])
    gy2 = send_y(2)
    given.append(give(gkv.at[1], gv_o))
    arrive([m_x, f1, f3, f2])
    wa0 = weights(0, gy0)
    wa1 = weights(1, gy1)
    wa2 = weights(2, gy2)
    partial()
    gxc = remote(gxs, gxr, mate)
    wb0 = second(0, wa0)
    wb1 = second(1, wa1)
    wb2 = second(2, wa2)
    wc0 = third(0, wb0)
    arrive([gxc])
    gx_o[...] = (gxf[...] + gxr[...].astype(F32)).astype(BF)
    wc1 = third(1, wb1)
    wc2 = third(2, wb2)
    assemble(0, wc0)
    assemble(1, wc1)
    assemble(2, wc2)
    arrive(given)
    assert count[0] <= SENDS and arrivals[0] <= LANDINGS, (count, arrivals)
    for copy in stored:
        copy.wait()
    for total, at in sent:
        pltpu.make_async_remote_copy(
            src_ref=total, dst_ref=total, send_sem=ssem.at[at], recv_sem=rsem.at[0], device_id=mate, device_id_type=MESH
        ).wait_send()


def hand_over(*refs):
    sources, outs, sem = refs[:5], refs[5:10], refs[10]
    copies = [pltpu.make_async_copy(src, out, sem.at[i]) for i, (src, out) in enumerate(zip(sources, outs))]
    for copy in copies:
        copy.start()
    for copy in copies:
        copy.wait()


def body(tokens, queries, values, key_weight, grad_out):
    anywhere = pl.BlockSpec(memory_space=pl.ANY)
    block = jax.ShapeDtypeStruct((TOK, D), BF)
    shapes = [block] * 4 + [jax.ShapeDtypeStruct((64, D), F32)]
    held = [pltpu.VMEM(shape.shape, shape.dtype) for shape in shapes]
    results = pl.pallas_call(
        kernel,
        out_shape=held,
        in_specs=[anywhere] * 6,
        out_specs=[pl.BlockSpec(memory_space=pltpu.VMEM)] * 5,
        scratch_shapes=[pltpu.VMEM(shape, dtype) for shape, dtype in SCRATCH.values()]
        + [pltpu.SemaphoreType.DMA((SENDS,)), pltpu.SemaphoreType.DMA((LANDINGS,))],
        compiler_params=pltpu.CompilerParams(
            collective_id=0, has_side_effects=True, vmem_limit_bytes=56 * 1024 * 1024
        ),
        name="hierarchical_attention",
    )(tokens[0], queries[0], values[0], key_weight, grad_out[0], jnp.asarray(matrices(), BF))
    att, gx, gq, gv, gw = pl.pallas_call(
        hand_over,
        out_shape=shapes,
        in_specs=[pl.BlockSpec(memory_space=pltpu.VMEM)] * 5,
        out_specs=[anywhere] * 5,
        scratch_shapes=[pltpu.SemaphoreType.DMA((5,))],
        name="hand_over",
    )(*[pltpu.with_memory_space_constraint(r, pltpu.VMEM) for r in results])
    return att[None], gx[None], gq[None], gv[None], gw


def solution(mesh):
    split = P("dp", "ctx", None)
    return jax.shard_map(
        body,
        mesh=mesh,
        in_specs=(split, split, split, P(), split),
        out_specs=(split, split, split, split, P("ctx", None)),
        check_vma=False,
    )
```

```python
import math

import jax
import jax.numpy as jnp
import numpy as np
from jax import lax
from jax.experimental import pallas as pl
from jax.experimental.pallas import tpu as pltpu
from jax.sharding import PartitionSpec as P

DH = 128
TOK = 128
D = 2048
HALF = D // 2
GROUPS = 4
GC = HALF // GROUPS
HEADS = 8
PARTS = ((0, 4), (4, 7), (7, 8))
SCALE = DH ** (-0.5)
BF = jnp.bfloat16
F32 = jnp.float32
MESH = pl.DeviceIdType.MESH
SENDS = 52
LANDINGS = 60


def matrices():
    pool = np.zeros((112, 432), np.float32)
    for tok in range(128):
        pool[tok // 2, tok] = 0.5
        pool[64 + tok // 4, tok] = 0.25
        pool[96 + tok // 8, tok] = 0.125
    rise = np.zeros((96, 432), np.float32)
    for row in range(64):
        rise[row // 4, row] = 0.25
        rise[64 + row // 8, row] = 0.125
        rise[16 + row // 4, 128 + row] = 0.25
        rise[72 + row // 8, 128 + row] = 0.125
        rise[32 + row // 2, 192 + row] = 0.5
        rise[80 + row // 4, 192 + row] = 0.25
    third = np.zeros((64, 432), np.float32)
    for row in range(64):
        third[row, row] = 1.0
        third[row, 64 + row // 2] = 0.5
        third[row, 96 + row // 2] = 0.5
    spread = np.zeros((256, 432), np.float32)
    for tok in range(256):
        spread[tok, tok // 2] = 0.5
        spread[tok, 128 + tok // 4] = 0.25
        spread[tok, 192 + tok // 8] = 0.125
        spread[tok, 224 + tok // 8] = 0.125
        for k in range(3):
            spread[tok, 256 + 16 * k + tok // 16] = 1 / 16
        spread[tok, 304:432] = third[tok // 16, :128] / 16
    return np.concatenate([pool, rise, third, spread], 0)


def flipped(place, k):
    if k == 0:
        return place
    if k == 1:
        return place + 1 - 2 * (place % 2)
    if k == 2:
        return place + 2 - 4 * (place // 2)
    return 3 - place


def nn(a, b):
    return lax.dot_general(a, b, (((1,), (0,)), ((), ())), preferred_element_type=F32)


def nt(a, b):
    return lax.dot_general(a, b, (((1,), (1,)), ((), ())), preferred_element_type=F32)


def tn(a, b):
    return lax.dot_general(a, b, (((0,), (0,)), ((), ())), preferred_element_type=F32)


SCRATCH = dict(
    xa=((4 * 256, D), BF),
    wv=((2, GROUPS, D, GC), BF),
    qv=((256, HALF), BF),
    gv=((256, HALF), BF),
    kl=((2, 192, HALF), BF),
    vl=((2, 192, HALF), BF),
    kt=((128, HALF), BF),
    vt=((128, HALF), BF),
    lo=((2, 64, HALF), BF),
    cc=((2, 256, HALF), BF),
    sp=((2, 2, 48, HALF), BF),
    sz=((2, 96, HALF), BF),
    dcb=((2, 256, HALF), BF),
    rb=((2, 432, HALF), BF),
    sx=((2, 64, HALF), BF),
    ld=((2, 256, HALF), F32),
    gkv=((2, 256, HALF), BF),
    ao=((256, HALF), BF),
    qo=((256, HALF), BF),
    gs=((HALF, 256), BF),
    gt0=((128, 1024), BF),
    gt1=((96, 1024), BF),
    gt2=((32, 1024), BF),
    rs0=((2, 4, 4, 64, 128), BF),
    rs1=((2, 4, 4, 48, 128), BF),
    rs2=((2, 4, 4, 16, 128), BF),
    ra0=((2, 3, 4, 64, 128), BF),
    ra1=((2, 3, 4, 48, 128), BF),
    ra2=((2, 3, 4, 16, 128), BF),
    tf0=((2, 4, 64, 128), F32),
    tf1=((2, 4, 48, 128), F32),
    tf2=((2, 4, 16, 128), F32),
    tb0=((2, 4, 64, 128), BF),
    tb1=((2, 4, 48, 128), BF),
    tb2=((2, 4, 16, 128), BF),
    rz0=((2, 3, 64, 128), BF),
    rz1=((2, 3, 48, 128), BF),
    rz2=((2, 3, 16, 128), BF),
    fo0=((128, 128), BF),
    fo1=((96, 128), BF),
    fo2=((32, 128), BF),
    ow0=((2, 4, 128, 128), BF),
    ow1=((2, 4, 96, 128), BF),
    ow2=((2, 4, 32, 128), BF),
    gxf=((128, D), F32),
    gxs=((128, D), BF),
    gxr=((128, D), BF),
    pp=((528, 432), BF),
)


def kernel(x_h, q_h, v_h, w_h, g_h, p_h, att_o, gx_o, gq_o, gv_o, gw_o, *rest):
    s = dict(zip(SCRATCH, rest[: len(SCRATCH)]))
    ssem, rsem = rest[len(SCRATCH) :]
    xa, wv, qv, gv, kl, vl, kt, vt, lo = (s[n] for n in ("xa", "wv", "qv", "gv", "kl", "vl", "kt", "vt", "lo"))
    cc, sp, sz, dcb, rb, sx, ld = (s[n] for n in ("cc", "sp", "sz", "dcb", "rb", "sx", "ld"))
    gkv, ao, qo, gs = (s[n] for n in ("gkv", "ao", "qo", "gs"))
    gt, rs, ra, tf, tb, rz, fo, ow = ([s[n + p] for p in "012"] for n in ("gt", "rs", "ra", "tf", "tb", "rz", "fo", "ow"))
    gxf, gxs, gxr, pp = (s[n] for n in ("gxf", "gxs", "gxr", "pp"))

    y = lax.axis_index("dp")
    ctx = lax.axis_index("ctx")
    core = ctx % 2
    xx = (ctx // 2) % 4
    zz = ctx // 8
    mate = (y, ctx + 1 - 2 * core)
    along_x = [(y, zz * 8 + flipped(xx, k) * 2 + core) for k in range(4)]
    cross_x = [(y, zz * 8 + flipped(xx, k) * 2 + 1 - core) for k in range(4)]
    along_z = [(y, flipped(zz, k) * 8 + xx * 2 + core) for k in range(4)]
    along_y = [(flipped(y, k), ctx) for k in range(4)]
    cross_y = [(flipped(y, k), mate[1]) for k in range(4)]
    mine = pl.multiple_of(core * HALF, HALF)
    theirs = pl.multiple_of((1 - core) * HALF, HALF)

    peers = [mate] + along_x[1:] + cross_x[1:] + along_z[1:] + along_y[1:] + cross_y[1:]
    barrier = pltpu.get_barrier_semaphore()
    for peer in peers:
        pl.semaphore_signal(barrier, inc=1, device_id=peer, device_id_type=MESH)

    count = [0]
    arrivals = [0]
    sent = []
    stored = []

    class Landing:
        def __init__(self, whole, send_at):
            self.at = arrivals[0]
            self.copy = pltpu.make_async_remote_copy(
                src_ref=whole,
                dst_ref=whole,
                send_sem=ssem.at[send_at],
                recv_sem=rsem.at[arrivals[0]],
                device_id=mate,
                device_id_type=MESH,
            )
            arrivals[0] += 1

    def start(src, dst, device, send_at, recv_at):
        pltpu.make_async_remote_copy(
            src_ref=src, dst_ref=dst, send_sem=ssem.at[send_at], recv_sem=rsem.at[recv_at], device_id=device, device_id_type=MESH
        ).start()

    class Route:
        def __init__(self, total):
            self.at = count[0]
            count[0] += 1
            sent.append((total, self.at))

        def send(self, whole, messages):
            return self.add(Landing(whole, self.at), messages)

        def add(self, landing, messages):
            for src, dst, device in messages:
                start(src, dst, device, self.at, landing.at)
            return landing

    def remote(src, dst, device):
        return Route(dst).send(dst, [(src, dst, device)])

    def local(src, dst):
        at = count[0]
        count[0] += 1
        copy = pltpu.make_async_copy(src, dst, ssem.at[at])
        copy.start()
        return copy

    def arrive(copies):
        for copy in copies:
            copy.copy.wait_recv()

    def cols(j):
        return pl.ds(j * GC, GC)

    def head_cols(i):
        return pl.ds(i * DH, DH)

    in_x = local(x_h, xa.at[0:128])
    in_p = local(p_h, pp)
    in_v = [local(v_h.at[:, pl.ds(mine, HALF)], vl.at[0, 0:128]), local(v_h.at[:, pl.ds(theirs, HALF)], vt)]
    in_w = [
        [local(w_h.at[:, pl.ds(pl.multiple_of(side + j * GC, GC), GC)], wv.at[h, j]) for h, side in enumerate((mine, theirs))]
        for j in range(GROUPS)
    ]
    in_q = local(q_h.at[:, pl.ds(mine, HALF)], qv.at[0:128])
    in_g = local(g_h.at[:, pl.ds(mine, HALF)], gv.at[0:128])

    def pooled(kv, ref, h, j, rows_in):
        rows = nn(pp[0:112, 0:128], rows_in).astype(BF)
        sp[h, kv, :, cols(j)] = rows[64:112]
        if h == 0:
            ref[1, 128:192, cols(j)] = rows[0:64]
            lo[kv, 0:32, cols(j)] = rows[64:96]

    in_p.wait()
    for copy in in_v:
        copy.wait()
    for j in range(GROUPS):
        pooled(1, vl, 0, j, vl[0, 0:128, cols(j)])
        pooled(1, vl, 1, j, vt[:, cols(j)])
    in_x.wait()
    for j in range(GROUPS):
        for h in (0, 1):
            in_w[j][h].wait()
            keys = nn(xa[0:128, :], wv[h, j]).astype(BF)
            if h == 0:
                kl[0, 0:128, cols(j)] = keys
            else:
                kt[:, cols(j)] = keys
            pooled(0, kl, h, j, keys)

    pl.semaphore_wait(barrier, len(peers))
    fx_route, fz_route = Route(cc.at[:, 0:128]), Route(cc.at[:, 128:256])
    bx_route, bz_route = Route(rb.at[:, 128:304]), Route(rb.at[:, 304:432])

    def send_x(i):
        at = head_cols(i)
        messages = []
        for h, line in ((0, along_x), (1, cross_x)):
            first = sp.at[h, :, 0:32, at]
            second = sp.at[h, :, 32:48, at]
            messages.append((second, cc.at[:, 64 + 16 * h : 80 + 16 * h, at], line[2]))
            messages.append((first, cc.at[:, 32 * h : 32 * h + 32, at], line[1]))
            messages.append((second, cc.at[:, 96 + 16 * h : 112 + 16 * h, at], line[3]))
        return fx_route.send(cc.at[:, 0:128, at], messages)

    fx = [send_x(0)]
    m_k = remote(kt, kl.at[1, 0:128], mate)
    m_v = remote(vt, vl.at[1, 0:128], mate)
    for i in range(1, HEADS):
        fx.append(send_x(i))
    y_x = {k: remote(x_h, xa.at[k * 256 : k * 256 + 128], along_y[k]) for k in (1, 3)}
    m_q = remote(q_h.at[:, pl.ds(theirs, HALF)], qv.at[128:256], mate)
    m_g = remote(g_h.at[:, pl.ds(theirs, HALF)], gv.at[128:256], mate)
    m_x = remote(x_h, xa.at[128:256], mate)

    arrive([m_k, m_v])
    for kv, ref in ((0, kl), (1, vl)):
        for j in range(GROUPS):
            rows = nn(pp[0:96, 0:128], ref[1, 0:128, cols(j)]).astype(BF)
            ref[0, 128:192, cols(j)] = rows[0:64]
            lo[kv, 32:64, cols(j)] = rows[64:96]

    def rise(i):
        arrive([fx[i]])
        at = head_cols(i)
        for kv in (0, 1):
            rows = nn(pp[112:208, 0:64], lo[kv, :, at]) + nn(pp[112:208, 128:256], cc[kv, 0:128, at])
            sz[kv, :, at] = rows.astype(BF)
        return fz_route.send(
            cc.at[:, 128:256, at],
            [
                (sz.at[:, 64:96, at], cc.at[:, 192:224, at], along_z[2]),
                (sz.at[:, 0:64, at], cc.at[:, 128:192, at], along_z[1]),
                (sz.at[:, 64:96, at], cc.at[:, 224:256, at], along_z[3]),
            ],
        )

    def head(c):
        q = qv[:, c]
        g = gv[:, c]
        ck = cc[0, :, c]
        cv = cc[1, :, c]
        rate = SCALE * math.log2(math.e)
        e1 = jnp.exp2(nt(q, ck) * rate)
        total = jnp.sum(e1, -1, keepdims=True)
        pair = [slice(0, 128), slice(128, 256)]
        e0 = [jnp.exp2(nt(q[pair[b]], kl[b, :, c]) * rate) for b in (0, 1)]
        total = total + jnp.concatenate([jnp.sum(e, -1, keepdims=True) for e in e0], 0)
        inverse = 1.0 / (total * 0.25)
        p1 = e1 * inverse
        p0 = [e0[b] * inverse[pair[b]] for b in (0, 1)]
        p1b = p1.astype(BF)
        p0b = [p.astype(BF) for p in p0]
        out = (nn(p1b, cv) + jnp.concatenate([nn(p0b[b], vl[b, :, c]) for b in (0, 1)], 0)) * 0.25
        ao[:, c] = out.astype(BF)
        delta = jnp.sum(g.astype(F32) * out, -1, keepdims=True)
        d1 = (p1 * (nt(g, cv) - delta)).astype(BF)
        d0 = [(p0[b] * (nt(g[pair[b]], vl[b, :, c]) - delta[pair[b]])).astype(BF) for b in (0, 1)]
        fold = SCALE * 0.25
        dq = (nn(d1, ck) + jnp.concatenate([nn(d0[b], kl[b, :, c]) for b in (0, 1)], 0)) * fold
        qo[:, c] = dq.astype(BF)
        dck = tn(d1, q) * fold
        dcv = tn(p1b, g) * 0.25
        dcb[0, :, c] = dck.astype(BF)
        dcb[1, :, c] = dcv.astype(BF)
        for b in (0, 1):
            dk = tn(d0[b], q[pair[b]]) * fold
            dv = tn(p0b[b], g[pair[b]]) * 0.25
            ld[0, pair[b], c] = dk[0:128]
            ld[1, pair[b], c] = dv[0:128]
            other = slice(64 - 64 * b, 128 - 64 * b)
            rb[0, other, c] = dk[128:192].astype(BF)
            rb[1, other, c] = dv[128:192].astype(BF)

    def attend(i, landing):
        arrive([landing])
        at = head_cols(i)
        head(at)
        along = bz_route.send(
            rb.at[:, 304:432, at],
            [
                (dcb.at[:, 192:224, at], rb.at[:, 368:400, at], along_z[2]),
                (dcb.at[:, 128:192, at], rb.at[:, 304:368, at], along_z[1]),
                (dcb.at[:, 224:256, at], rb.at[:, 400:432, at], along_z[3]),
            ],
        )
        across = bx_route.send(
            rb.at[:, 128:304, at],
            [
                (dcb.at[:, 64:96, at], rb.at[:, 192:224, at], along_x[2]),
                (dcb.at[:, 0:64, at], rb.at[:, 128:192, at], along_x[1]),
                (dcb.at[:, 96:128, at], rb.at[:, 224:256, at], along_x[3]),
            ],
        )
        return along, across

    def return_x(i, landings):
        along, across = landings
        arrive([along])
        at = head_cols(i)
        for kv in (0, 1):
            sx[kv, :, at] = nn(pp[208:272, 0:128], rb[kv, 304:432, at]).astype(BF)
        return bx_route.add(
            across, [(sx.at[:, 16 * k : 16 * k + 16, at], rb.at[:, 240 + 16 * k : 256 + 16 * k, at], along_x[k]) for k in (2, 1, 3)]
        )

    def finish(i, landing):
        arrive([landing])
        at = head_cols(i)
        for kv in (0, 1):
            total = ld[kv, :, at] + nn(pp[272:528, :], rb[kv, :, at])
            gkv[kv, :, at] = total.astype(BF)
            if kv == 0:
                gs[at, :] = total.T.astype(BF)

    def send_y(p):
        first, last = PARTS[p]
        each = (last - first) * 32
        quarter = [pl.ds(pl.multiple_of(first * DH + flipped(y, k) * each, 32), each) for k in range(4)]
        landing = Route(gt[p].at[:, 256:1024]).send(
            gt[p].at[:, 256:1024],
            [(gs.at[quarter[k]], gt[p].at[:, k * 256 : (k + 1) * 256], along_y[k]) for k in (2, 1, 3)],
        )
        gt[p][:, 0:256] = gs[quarter[0], :]
        return landing

    def forward(k):
        arrive([y_x[k]])
        rows = 0 if k == 1 else 64
        ahead = remote(xa.at[k * 256 + rows : k * 256 + rows + 64], xa.at[512 + rows : 512 + rows + 64], along_y[4 - k])
        return remote(xa.at[k * 256 : k * 256 + 128], xa.at[k * 256 + 128 : k * 256 + 256], mate), ahead

    lines = ((xx, along_x), (zz, along_z))

    def weights(p, landing):
        arrive([landing])
        each = rs[p].shape[3]

        columns = gt[p][...]
        for i in range(8):
            part = nn(columns, xa[:, i * 256 : i * 256 + 256]).astype(BF)
            for n in (0, 1):
                x_at = 2 * (i % 2) + n
                rs[p][0, x_at, i // 2] = part[0:each, n * 128 : n * 128 + 128]
                rs[p][1, i // 2, x_at] = part[each : 2 * each, n * 128 : n * 128 + 128]
        return Route(ra[p]).send(
            ra[p],
            [
                (rs[p].at[d, flipped(lines[d][0], k)], ra[p].at[d, k - 1], lines[d][1][k])
                for k in (2, 1, 3)
                for d in (0, 1)
            ],
        )

    def second(p, landing):
        arrive([landing])
        messages = []
        for d in (0, 1):
            total = rs[p][d, lines[d][0]].astype(F32)
            for k in range(3):
                total = total + ra[p][d, k].astype(F32)
            tf[p][d] = total
            tb[p][d] = total.astype(BF)
            place, line = lines[1 - d]
            messages += [(tb[p].at[d, flipped(place, k)], rz[p].at[d, k - 1], line[k]) for k in (2, 1, 3)]
        return Route(rz[p]).send(rz[p], messages)

    def third(p, landing):
        arrive([landing])
        each = rs[p].shape[3]
        for d in (0, 1):
            total = tf[p][d, lines[1 - d][0]]
            for k in range(3):
                total = total + rz[p][d, k].astype(F32)
            fo[p][d * each : d * each + each] = total.astype(BF)
        whole = xa.at[0 : 7 * each, 0:256]
        landing = Route(whole).send(
            whole,
            [(fo[p], ow[p].at[core, y], along_y[k]) for k in (2, 1, 3)]
            + [(fo[p], ow[p].at[core, y], cross_y[k]) for k in (2, 1, 3, 0)],
        )
        ow[p][core, y] = fo[p][...]
        return landing

    def assemble(p, landing):
        arrive([landing])
        first, last = PARTS[p]
        wide = (last - first) * DH
        for side in (0, 1):
            turned = ow[p][side].astype(F32).reshape(wide, 128).T
            gw_o[:, pl.ds(side * HALF + first * DH, wide)] = jnp.where(core == 0, turned[0:64], turned[64:128])

    def give(staged, out):
        stored.append(local(staged.at[0:128], out.at[:, pl.ds(mine, HALF)]))
        return remote(staged.at[128:256], out.at[:, pl.ds(mine, HALF)], mate)

    def partial():
        for i in range(8):
            at = pl.ds(i * 256, 256)
            total = nt(gkv[0, :, cols(0)], wv[0, 0, at, :])
            for j in range(1, GROUPS):
                total = total + nt(gkv[0, :, cols(j)], wv[0, j, at, :])
            gxf[:, at] = total[0:128]
            gxs[:, at] = total[128:256].astype(BF)

    fz = [rise(i) for i in range(7)]
    in_q.wait()
    in_g.wait()
    arrive([m_q, m_g])
    bz, bx = [], []
    for i in range(4):
        bz.append(attend(i, fz[i]))
        if i < 1:
            fz.append(rise(7 + i))
    f1, a1 = forward(1)
    f3, a3 = forward(3)
    bz.append(attend(4, fz[4]))
    bz.append(attend(5, fz[5]))
    bx.append(return_x(0, bz[0]))
    bz.append(attend(6, fz[6]))
    bx.append(return_x(1, bz[1]))
    bz.append(attend(7, fz[7]))
    given = [give(ao, att_o), give(qo, gq_o)]
    bx.append(return_x(2, bz[2]))
    bx.append(return_x(3, bz[3]))
    finish(0, bx[0])
    bx.append(return_x(4, bz[4]))
    finish(1, bx[1])
    bx.append(return_x(5, bz[5]))
    finish(2, bx[2])
    bx.append(return_x(6, bz[6]))
    finish(3, bx[3])
    gy0 = send_y(0)
    bx.append(return_x(7, bz[7]))
    arrive([a1, a3])
    f2 = remote(xa.at[512:640], xa.at[640:768], mate)
    finish(4, bx[4])
    finish(5, bx[5])
    finish(6, bx[6])
    gy1 = send_y(1)
    finish(7, bx[7])
    gy2 = send_y(2)
    given.append(give(gkv.at[1], gv_o))
    arrive([m_x, f1, f3, f2])
    wa0 = weights(0, gy0)
    wa1 = weights(1, gy1)
    wa2 = weights(2, gy2)
    partial()
    gxc = remote(gxs, gxr, mate)
    wb0 = second(0, wa0)
    wb1 = second(1, wa1)
    wb2 = second(2, wa2)
    wc0 = third(0, wb0)
    arrive([gxc])
    gx_o[...] = (gxf[...] + gxr[...].astype(F32)).astype(BF)
    wc1 = third(1, wb1)
    wc2 = third(2, wb2)
    assemble(0, wc0)
    assemble(1, wc1)
    assemble(2, wc2)
    arrive(given)
    assert count[0] <= SENDS and arrivals[0] <= LANDINGS, (count, arrivals)
    for copy in stored:
        copy.wait()
    for total, at in sent:
        pltpu.make_async_remote_copy(
            src_ref=total, dst_ref=total, send_sem=ssem.at[at], recv_sem=rsem.at[0], device_id=mate, device_id_type=MESH
        ).wait_send()


def hand_over(*refs):
    sources, outs, sem = refs[:5], refs[5:10], refs[10]
    copies = [pltpu.make_async_copy(src, out, sem.at[i]) for i, (src, out) in enumerate(zip(sources, outs))]
    for copy in copies:
        copy.start()
    for copy in copies:
        copy.wait()


def body(tokens, queries, values, key_weight, grad_out):
    anywhere = pl.BlockSpec(memory_space=pl.ANY)
    block = jax.ShapeDtypeStruct((TOK, D), BF)
    shapes = [block] * 4 + [jax.ShapeDtypeStruct((64, D), F32)]
    held = [pltpu.VMEM(shape.shape, shape.dtype) for shape in shapes]
    results = pl.pallas_call(
        kernel,
        out_shape=held,
        in_specs=[anywhere] * 6,
        out_specs=[pl.BlockSpec(memory_space=pltpu.VMEM)] * 5,
        scratch_shapes=[pltpu.VMEM(shape, dtype) for shape, dtype in SCRATCH.values()]
        + [pltpu.SemaphoreType.DMA((SENDS,)), pltpu.SemaphoreType.DMA((LANDINGS,))],
        compiler_params=pltpu.CompilerParams(
            collective_id=0, has_side_effects=True, vmem_limit_bytes=56 * 1024 * 1024
        ),
        name="hierarchical_attention",
    )(tokens[0], queries[0], values[0], key_weight, grad_out[0], jnp.asarray(matrices(), BF))
    att, gx, gq, gv, gw = pl.pallas_call(
        hand_over,
        out_shape=shapes,
        in_specs=[pl.BlockSpec(memory_space=pltpu.VMEM)] * 5,
        out_specs=[anywhere] * 5,
        scratch_shapes=[pltpu.SemaphoreType.DMA((5,))],
        name="hand_over",
    )(*[pltpu.with_memory_space_constraint(r, pltpu.VMEM) for r in results])
    return att[None], gx[None], gq[None], gv[None], gw


def solution(mesh):
    split = P("dp", "ctx", None)
    return jax.shard_map(
        body,
        mesh=mesh,
        in_specs=(split, split, split, P(), split),
        out_specs=(split, split, split, split, P("ctx", None)),
        check_vma=False,
    )
```

```python
import math

import jax
import jax.numpy as jnp
import numpy as np
from jax import lax
from jax.experimental import pallas as pl
from jax.experimental.pallas import tpu as pltpu
from jax.sharding import PartitionSpec as P

DH = 128
TOK = 128
D = 2048
HALF = D // 2
GROUPS = 4
GC = HALF // GROUPS
HEADS = 8
PARTS = ((0, 4), (4, 7), (7, 8))
SCALE = DH ** (-0.5)
BF = jnp.bfloat16
F32 = jnp.float32
MESH = pl.DeviceIdType.MESH
SENDS = 52
LANDINGS = 60


def matrices():
    pool = np.zeros((112, 432), np.float32)
    for tok in range(128):
        pool[tok // 2, tok] = 0.5
        pool[64 + tok // 4, tok] = 0.25
        pool[96 + tok // 8, tok] = 0.125
    rise = np.zeros((96, 432), np.float32)
    for row in range(64):
        rise[row // 4, row] = 0.25
        rise[64 + row // 8, row] = 0.125
        rise[16 + row // 4, 128 + row] = 0.25
        rise[72 + row // 8, 128 + row] = 0.125
        rise[32 + row // 2, 192 + row] = 0.5
        rise[80 + row // 4, 192 + row] = 0.25
    third = np.zeros((64, 432), np.float32)
    for row in range(64):
        third[row, row] = 1.0
        third[row, 64 + row // 2] = 0.5
        third[row, 96 + row // 2] = 0.5
    spread = np.zeros((256, 432), np.float32)
    for tok in range(256):
        spread[tok, tok // 2] = 0.5
        spread[tok, 128 + tok // 4] = 0.25
        spread[tok, 192 + tok // 8] = 0.125
        spread[tok, 224 + tok // 8] = 0.125
        for k in range(3):
            spread[tok, 256 + 16 * k + tok // 16] = 1 / 16
        spread[tok, 304:432] = third[tok // 16, :128] / 16
    return np.concatenate([pool, rise, third, spread], 0)


def flipped(place, k):
    if k == 0:
        return place
    if k == 1:
        return place + 1 - 2 * (place % 2)
    if k == 2:
        return place + 2 - 4 * (place // 2)
    return 3 - place


def nn(a, b):
    return lax.dot_general(a, b, (((1,), (0,)), ((), ())), preferred_element_type=F32)


def nt(a, b):
    return lax.dot_general(a, b, (((1,), (1,)), ((), ())), preferred_element_type=F32)


def tn(a, b):
    return lax.dot_general(a, b, (((0,), (0,)), ((), ())), preferred_element_type=F32)


SCRATCH = dict(
    xa=((4 * 256, D), BF),
    wv=((2, GROUPS, D, GC), BF),
    qv=((256, HALF), BF),
    gv=((256, HALF), BF),
    kl=((2, 192, HALF), BF),
    vl=((2, 192, HALF), BF),
    kt=((128, HALF), BF),
    vt=((128, HALF), BF),
    lo=((2, 64, HALF), BF),
    cc=((2, 256, HALF), BF),
    sp=((2, 2, 48, HALF), BF),
    sz=((2, 96, HALF), BF),
    dcb=((2, 256, HALF), BF),
    rb=((2, 432, HALF), BF),
    sx=((2, 64, HALF), BF),
    ld=((2, 256, HALF), F32),
    gkv=((2, 256, HALF), BF),
    ao=((256, HALF), BF),
    qo=((256, HALF), BF),
    gs=((HALF, 256), BF),
    gt0=((128, 1024), BF),
    gt1=((96, 1024), BF),
    gt2=((32, 1024), BF),
    rs0=((2, 4, 4, 64, 128), BF),
    rs1=((2, 4, 4, 48, 128), BF),
    rs2=((2, 4, 4, 16, 128), BF),
    ra0=((2, 3, 4, 64, 128), BF),
    ra1=((2, 3, 4, 48, 128), BF),
    ra2=((2, 3, 4, 16, 128), BF),
    tf0=((2, 4, 64, 128), F32),
    tf1=((2, 4, 48, 128), F32),
    tf2=((2, 4, 16, 128), F32),
    tb0=((2, 4, 64, 128), BF),
    tb1=((2, 4, 48, 128), BF),
    tb2=((2, 4, 16, 128), BF),
    rz0=((2, 3, 64, 128), BF),
    rz1=((2, 3, 48, 128), BF),
    rz2=((2, 3, 16, 128), BF),
    fo0=((128, 128), BF),
    fo1=((96, 128), BF),
    fo2=((32, 128), BF),
    ow0=((2, 4, 128, 128), BF),
    ow1=((2, 4, 96, 128), BF),
    ow2=((2, 4, 32, 128), BF),
    gxf=((128, D), F32),
    gxs=((128, D), BF),
    gxr=((128, D), BF),
    pp=((528, 432), BF),
)


def kernel(x_h, q_h, v_h, w_h, g_h, p_h, att_o, gx_o, gq_o, gv_o, gw_o, *rest):
    s = dict(zip(SCRATCH, rest[: len(SCRATCH)]))
    ssem, rsem = rest[len(SCRATCH) :]
    xa, wv, qv, gv, kl, vl, kt, vt, lo = (s[n] for n in ("xa", "wv", "qv", "gv", "kl", "vl", "kt", "vt", "lo"))
    cc, sp, sz, dcb, rb, sx, ld = (s[n] for n in ("cc", "sp", "sz", "dcb", "rb", "sx", "ld"))
    gkv, ao, qo, gs = (s[n] for n in ("gkv", "ao", "qo", "gs"))
    gt, rs, ra, tf, tb, rz, fo, ow = ([s[n + p] for p in "012"] for n in ("gt", "rs", "ra", "tf", "tb", "rz", "fo", "ow"))
    gxf, gxs, gxr, pp = (s[n] for n in ("gxf", "gxs", "gxr", "pp"))

    y = lax.axis_index("dp")
    ctx = lax.axis_index("ctx")
    core = ctx % 2
    xx = (ctx // 2) % 4
    zz = ctx // 8
    mate = (y, ctx + 1 - 2 * core)
    along_x = [(y, zz * 8 + flipped(xx, k) * 2 + core) for k in range(4)]
    cross_x = [(y, zz * 8 + flipped(xx, k) * 2 + 1 - core) for k in range(4)]
    along_z = [(y, flipped(zz, k) * 8 + xx * 2 + core) for k in range(4)]
    along_y = [(flipped(y, k), ctx) for k in range(4)]
    cross_y = [(flipped(y, k), mate[1]) for k in range(4)]
    mine = pl.multiple_of(core * HALF, HALF)
    theirs = pl.multiple_of((1 - core) * HALF, HALF)

    peers = [mate] + along_x[1:] + cross_x[1:] + along_z[1:] + along_y[1:] + cross_y[1:]
    barrier = pltpu.get_barrier_semaphore()
    for peer in peers:
        pl.semaphore_signal(barrier, inc=1, device_id=peer, device_id_type=MESH)

    count = [0]
    arrivals = [0]
    sent = []
    stored = []

    class Landing:
        def __init__(self, whole, send_at):
            self.at = arrivals[0]
            self.copy = pltpu.make_async_remote_copy(
                src_ref=whole,
                dst_ref=whole,
                send_sem=ssem.at[send_at],
                recv_sem=rsem.at[arrivals[0]],
                device_id=mate,
                device_id_type=MESH,
            )
            arrivals[0] += 1

    def start(src, dst, device, send_at, recv_at):
        pltpu.make_async_remote_copy(
            src_ref=src, dst_ref=dst, send_sem=ssem.at[send_at], recv_sem=rsem.at[recv_at], device_id=device, device_id_type=MESH
        ).start()

    class Route:
        def __init__(self, total):
            self.at = count[0]
            count[0] += 1
            sent.append((total, self.at))

        def send(self, whole, messages):
            return self.add(Landing(whole, self.at), messages)

        def add(self, landing, messages):
            for src, dst, device in messages:
                start(src, dst, device, self.at, landing.at)
            return landing

    def remote(src, dst, device):
        return Route(dst).send(dst, [(src, dst, device)])

    def local(src, dst):
        at = count[0]
        count[0] += 1
        copy = pltpu.make_async_copy(src, dst, ssem.at[at])
        copy.start()
        return copy

    def arrive(copies):
        for copy in copies:
            copy.copy.wait_recv()

    def cols(j):
        return pl.ds(j * GC, GC)

    def head_cols(i):
        return pl.ds(i * DH, DH)

    in_x = local(x_h, xa.at[0:128])
    in_p = local(p_h, pp)
    in_v = [local(v_h.at[:, pl.ds(mine, HALF)], vl.at[0, 0:128]), local(v_h.at[:, pl.ds(theirs, HALF)], vt)]
    in_w = [
        [local(w_h.at[:, pl.ds(pl.multiple_of(side + j * GC, GC), GC)], wv.at[h, j]) for h, side in enumerate((mine, theirs))]
        for j in range(GROUPS)
    ]
    in_q = local(q_h.at[:, pl.ds(mine, HALF)], qv.at[0:128])
    in_g = local(g_h.at[:, pl.ds(mine, HALF)], gv.at[0:128])

    def pooled(kv, ref, h, j, rows_in):
        rows = nn(pp[0:112, 0:128], rows_in).astype(BF)
        sp[h, kv, :, cols(j)] = rows[64:112]
        if h == 0:
            ref[1, 128:192, cols(j)] = rows[0:64]
            lo[kv, 0:32, cols(j)] = rows[64:96]

    in_p.wait()
    for copy in in_v:
        copy.wait()
    for j in range(GROUPS):
        pooled(1, vl, 0, j, vl[0, 0:128, cols(j)])
        pooled(1, vl, 1, j, vt[:, cols(j)])
    in_x.wait()
    for j in range(GROUPS):
        for h in (0, 1):
            in_w[j][h].wait()
            keys = nn(xa[0:128, :], wv[h, j]).astype(BF)
            if h == 0:
                kl[0, 0:128, cols(j)] = keys
            else:
                kt[:, cols(j)] = keys
            pooled(0, kl, h, j, keys)

    pl.semaphore_wait(barrier, len(peers))
    fx_route, fz_route = Route(cc.at[:, 0:128]), Route(cc.at[:, 128:256])
    bx_route, bz_route = Route(rb.at[:, 128:304]), Route(rb.at[:, 304:432])

    def send_x(i):
        at = head_cols(i)
        messages = []
        for h, line in ((0, along_x), (1, cross_x)):
            first = sp.at[h, :, 0:32, at]
            second = sp.at[h, :, 32:48, at]
            messages.append((second, cc.at[:, 64 + 16 * h : 80 + 16 * h, at], line[2]))
            messages.append((first, cc.at[:, 32 * h : 32 * h + 32, at], line[1]))
            messages.append((second, cc.at[:, 96 + 16 * h : 112 + 16 * h, at], line[3]))
        return fx_route.send(cc.at[:, 0:128, at], messages)

    fx = [send_x(0)]
    m_k = remote(kt, kl.at[1, 0:128], mate)
    m_v = remote(vt, vl.at[1, 0:128], mate)
    for i in range(1, HEADS):
        fx.append(send_x(i))
    y_x = {k: remote(x_h, xa.at[k * 256 : k * 256 + 128], along_y[k]) for k in (1, 3)}
    m_q = remote(q_h.at[:, pl.ds(theirs, HALF)], qv.at[128:256], mate)
    m_g = remote(g_h.at[:, pl.ds(theirs, HALF)], gv.at[128:256], mate)
    m_x = remote(x_h, xa.at[128:256], mate)

    arrive([m_k, m_v])
    for kv, ref in ((0, kl), (1, vl)):
        for j in range(GROUPS):
            rows = nn(pp[0:96, 0:128], ref[1, 0:128, cols(j)]).astype(BF)
            ref[0, 128:192, cols(j)] = rows[0:64]
            lo[kv, 32:64, cols(j)] = rows[64:96]

    def rise(i):
        arrive([fx[i]])
        at = head_cols(i)
        for kv in (0, 1):
            rows = nn(pp[112:208, 0:64], lo[kv, :, at]) + nn(pp[112:208, 128:256], cc[kv, 0:128, at])
            sz[kv, :, at] = rows.astype(BF)
        return fz_route.send(
            cc.at[:, 128:256, at],
            [
                (sz.at[:, 64:96, at], cc.at[:, 192:224, at], along_z[2]),
                (sz.at[:, 0:64, at], cc.at[:, 128:192, at], along_z[1]),
                (sz.at[:, 64:96, at], cc.at[:, 224:256, at], along_z[3]),
            ],
        )

    def head(c, send):
        q = qv[:, c]
        g = gv[:, c]
        ck = cc[0, :, c]
        cv = cc[1, :, c]
        rate = SCALE * math.log2(math.e)
        e1 = jnp.exp2(nt(q, ck) * rate)
        total = jnp.sum(e1, -1, keepdims=True)
        pair = [slice(0, 128), slice(128, 256)]
        e0 = [jnp.exp2(nt(q[pair[b]], kl[b, :, c]) * rate) for b in (0, 1)]
        total = total + jnp.concatenate([jnp.sum(e, -1, keepdims=True) for e in e0], 0)
        inverse = 1.0 / (total * 0.25)
        p1 = e1 * inverse
        p0 = [e0[b] * inverse[pair[b]] for b in (0, 1)]
        p1b = p1.astype(BF)
        p0b = [p.astype(BF) for p in p0]
        out = (nn(p1b, cv) + jnp.concatenate([nn(p0b[b], vl[b, :, c]) for b in (0, 1)], 0)) * 0.25
        ao[:, c] = out.astype(BF)
        delta = jnp.sum(g.astype(F32) * out, -1, keepdims=True)
        d1 = (p1 * (nt(g, cv) - delta)).astype(BF)
        d0 = [(p0[b] * (nt(g[pair[b]], vl[b, :, c]) - delta[pair[b]])).astype(BF) for b in (0, 1)]
        fold = SCALE * 0.25
        dq = (nn(d1, ck) + jnp.concatenate([nn(d0[b], kl[b, :, c]) for b in (0, 1)], 0)) * fold
        qo[:, c] = dq.astype(BF)
        dck = tn(d1, q) * fold
        dcv = tn(p1b, g) * 0.25
        dcb[0, :, c] = dck.astype(BF)
        dcb[1, :, c] = dcv.astype(BF)
        landings = send()
        for b in (0, 1):
            dk = tn(d0[b], q[pair[b]]) * fold
            dv = tn(p0b[b], g[pair[b]]) * 0.25
            ld[0, pair[b], c] = dk[0:128]
            ld[1, pair[b], c] = dv[0:128]
            other = slice(64 - 64 * b, 128 - 64 * b)
            rb[0, other, c] = dk[128:192].astype(BF)
            rb[1, other, c] = dv[128:192].astype(BF)
        return landings

    def attend(i, landing):
        arrive([landing])
        at = head_cols(i)

        def send():
            along = bz_route.send(
                rb.at[:, 304:432, at],
                [
                    (dcb.at[:, 192:224, at], rb.at[:, 368:400, at], along_z[2]),
                    (dcb.at[:, 128:192, at], rb.at[:, 304:368, at], along_z[1]),
                    (dcb.at[:, 224:256, at], rb.at[:, 400:432, at], along_z[3]),
                ],
            )
            across = bx_route.send(
                rb.at[:, 128:304, at],
                [
                    (dcb.at[:, 64:96, at], rb.at[:, 192:224, at], along_x[2]),
                    (dcb.at[:, 0:64, at], rb.at[:, 128:192, at], along_x[1]),
                    (dcb.at[:, 96:128, at], rb.at[:, 224:256, at], along_x[3]),
                ],
            )
            return along, across

        return head(at, send)

    def return_x(i, landings):
        along, across = landings
        arrive([along])
        at = head_cols(i)
        for kv in (0, 1):
            sx[kv, :, at] = nn(pp[208:272, 0:128], rb[kv, 304:432, at]).astype(BF)
        return bx_route.add(
            across, [(sx.at[:, 16 * k : 16 * k + 16, at], rb.at[:, 240 + 16 * k : 256 + 16 * k, at], along_x[k]) for k in (2, 1, 3)]
        )

    def finish(i, landing):
        arrive([landing])
        at = head_cols(i)
        for kv in (0, 1):
            total = ld[kv, :, at] + nn(pp[272:528, :], rb[kv, :, at])
            gkv[kv, :, at] = total.astype(BF)
            if kv == 0:
                gs[at, :] = total.T.astype(BF)

    def send_y(p):
        first, last = PARTS[p]
        each = (last - first) * 32
        quarter = [pl.ds(pl.multiple_of(first * DH + flipped(y, k) * each, 32), each) for k in range(4)]
        landing = Route(gt[p].at[:, 256:1024]).send(
            gt[p].at[:, 256:1024],
            [(gs.at[quarter[k]], gt[p].at[:, k * 256 : (k + 1) * 256], along_y[k]) for k in (2, 1, 3)],
        )
        gt[p][:, 0:256] = gs[quarter[0], :]
        return landing

    def forward(k):
        arrive([y_x[k]])
        rows = 0 if k == 1 else 64
        ahead = remote(xa.at[k * 256 + rows : k * 256 + rows + 64], xa.at[512 + rows : 512 + rows + 64], along_y[4 - k])
        return remote(xa.at[k * 256 : k * 256 + 128], xa.at[k * 256 + 128 : k * 256 + 256], mate), ahead

    lines = ((xx, along_x), (zz, along_z))

    def weights(p, landing):
        arrive([landing])
        each = rs[p].shape[3]

        columns = gt[p][...]
        for i in range(8):
            part = nn(columns, xa[:, i * 256 : i * 256 + 256]).astype(BF)
            for n in (0, 1):
                x_at = 2 * (i % 2) + n
                rs[p][0, x_at, i // 2] = part[0:each, n * 128 : n * 128 + 128]
                rs[p][1, i // 2, x_at] = part[each : 2 * each, n * 128 : n * 128 + 128]
        return Route(ra[p]).send(
            ra[p],
            [
                (rs[p].at[d, flipped(lines[d][0], k)], ra[p].at[d, k - 1], lines[d][1][k])
                for k in (2, 1, 3)
                for d in (0, 1)
            ],
        )

    def second(p, landing):
        arrive([landing])
        messages = []
        for d in (0, 1):
            total = rs[p][d, lines[d][0]].astype(F32)
            for k in range(3):
                total = total + ra[p][d, k].astype(F32)
            tf[p][d] = total
            tb[p][d] = total.astype(BF)
            place, line = lines[1 - d]
            messages += [(tb[p].at[d, flipped(place, k)], rz[p].at[d, k - 1], line[k]) for k in (2, 1, 3)]
        return Route(rz[p]).send(rz[p], messages)

    def third(p, landing):
        arrive([landing])
        each = rs[p].shape[3]
        for d in (0, 1):
            total = tf[p][d, lines[1 - d][0]]
            for k in range(3):
                total = total + rz[p][d, k].astype(F32)
            fo[p][d * each : d * each + each] = total.astype(BF)
        whole = xa.at[0 : 7 * each, 0:256]
        landing = Route(whole).send(
            whole,
            [(fo[p], ow[p].at[core, y], along_y[k]) for k in (2, 1, 3)]
            + [(fo[p], ow[p].at[core, y], cross_y[k]) for k in (2, 1, 3, 0)],
        )
        ow[p][core, y] = fo[p][...]
        return landing

    def assemble(p, landing):
        arrive([landing])
        first, last = PARTS[p]
        wide = (last - first) * DH
        for side in (0, 1):
            turned = ow[p][side].astype(F32).reshape(wide, 128).T
            gw_o[:, pl.ds(side * HALF + first * DH, wide)] = jnp.where(core == 0, turned[0:64], turned[64:128])

    def give(staged, out):
        stored.append(local(staged.at[0:128], out.at[:, pl.ds(mine, HALF)]))
        return remote(staged.at[128:256], out.at[:, pl.ds(mine, HALF)], mate)

    def partial():
        for i in range(8):
            at = pl.ds(i * 256, 256)
            total = nt(gkv[0, :, cols(0)], wv[0, 0, at, :])
            for j in range(1, GROUPS):
                total = total + nt(gkv[0, :, cols(j)], wv[0, j, at, :])
            gxf[:, at] = total[0:128]
            gxs[:, at] = total[128:256].astype(BF)

    fz = [rise(i) for i in range(7)]
    in_q.wait()
    in_g.wait()
    arrive([m_q, m_g])
    bz, bx = [], []
    for i in range(4):
        bz.append(attend(i, fz[i]))
        if i < 1:
            fz.append(rise(7 + i))
    f1, a1 = forward(1)
    f3, a3 = forward(3)
    bz.append(attend(4, fz[4]))
    bz.append(attend(5, fz[5]))
    bx.append(return_x(0, bz[0]))
    bz.append(attend(6, fz[6]))
    bx.append(return_x(1, bz[1]))
    bz.append(attend(7, fz[7]))
    given = [give(ao, att_o), give(qo, gq_o)]
    bx.append(return_x(2, bz[2]))
    bx.append(return_x(3, bz[3]))
    finish(0, bx[0])
    bx.append(return_x(4, bz[4]))
    finish(1, bx[1])
    bx.append(return_x(5, bz[5]))
    finish(2, bx[2])
    bx.append(return_x(6, bz[6]))
    finish(3, bx[3])
    gy0 = send_y(0)
    bx.append(return_x(7, bz[7]))
    arrive([a1, a3])
    f2 = remote(xa.at[512:640], xa.at[640:768], mate)
    finish(4, bx[4])
    finish(5, bx[5])
    finish(6, bx[6])
    gy1 = send_y(1)
    finish(7, bx[7])
    gy2 = send_y(2)
    given.append(give(gkv.at[1], gv_o))
    arrive([m_x, f1, f3, f2])
    wa0 = weights(0, gy0)
    wa1 = weights(1, gy1)
    wa2 = weights(2, gy2)
    partial()
    gxc = remote(gxs, gxr, mate)
    wb0 = second(0, wa0)
    wb1 = second(1, wa1)
    wb2 = second(2, wa2)
    wc0 = third(0, wb0)
    arrive([gxc])
    gx_o[...] = (gxf[...] + gxr[...].astype(F32)).astype(BF)
    wc1 = third(1, wb1)
    wc2 = third(2, wb2)
    assemble(0, wc0)
    assemble(1, wc1)
    assemble(2, wc2)
    arrive(given)
    assert count[0] <= SENDS and arrivals[0] <= LANDINGS, (count, arrivals)
    for copy in stored:
        copy.wait()
    for total, at in sent:
        pltpu.make_async_remote_copy(
            src_ref=total, dst_ref=total, send_sem=ssem.at[at], recv_sem=rsem.at[0], device_id=mate, device_id_type=MESH
        ).wait_send()


def hand_over(*refs):
    sources, outs, sem = refs[:5], refs[5:10], refs[10]
    copies = [pltpu.make_async_copy(src, out, sem.at[i]) for i, (src, out) in enumerate(zip(sources, outs))]
    for copy in copies:
        copy.start()
    for copy in copies:
        copy.wait()


def body(tokens, queries, values, key_weight, grad_out):
    anywhere = pl.BlockSpec(memory_space=pl.ANY)
    block = jax.ShapeDtypeStruct((TOK, D), BF)
    shapes = [block] * 4 + [jax.ShapeDtypeStruct((64, D), F32)]
    held = [pltpu.VMEM(shape.shape, shape.dtype) for shape in shapes]
    results = pl.pallas_call(
        kernel,
        out_shape=held,
        in_specs=[anywhere] * 6,
        out_specs=[pl.BlockSpec(memory_space=pltpu.VMEM)] * 5,
        scratch_shapes=[pltpu.VMEM(shape, dtype) for shape, dtype in SCRATCH.values()]
        + [pltpu.SemaphoreType.DMA((SENDS,)), pltpu.SemaphoreType.DMA((LANDINGS,))],
        compiler_params=pltpu.CompilerParams(
            collective_id=0, has_side_effects=True, vmem_limit_bytes=56 * 1024 * 1024
        ),
        name="hierarchical_attention",
    )(tokens[0], queries[0], values[0], key_weight, grad_out[0], jnp.asarray(matrices(), BF))
    att, gx, gq, gv, gw = pl.pallas_call(
        hand_over,
        out_shape=shapes,
        in_specs=[pl.BlockSpec(memory_space=pltpu.VMEM)] * 5,
        out_specs=[anywhere] * 5,
        scratch_shapes=[pltpu.SemaphoreType.DMA((5,))],
        name="hand_over",
    )(*[pltpu.with_memory_space_constraint(r, pltpu.VMEM) for r in results])
    return att[None], gx[None], gq[None], gv[None], gw


def solution(mesh):
    split = P("dp", "ctx", None)
    return jax.shard_map(
        body,
        mesh=mesh,
        in_specs=(split, split, split, P(), split),
        out_specs=(split, split, split, split, P("ctx", None)),
        check_vma=False,
    )
```
